512 devices in a mesh: row: 16 (over y, x_lo, core), col: 32 (over z, x_hi).
Axes of the slice: x: 4 (x_hi: 2, x_lo: 2; x = x_hi * 2 + x_lo), y: 4, z: 16, core: 2. Of those that a mesh axis runs over, the one named last changes fastest.
Arguments:
- features: bfloat16 [65536, 128], P(('row', 'col')), may hold values from -6 to 6
- weight: bfloat16 [128, 128], replicated, may hold values from -0.5 to 0.5
- bias: float32 [128], replicated, may hold values from -3 to 3
- tile_values: bfloat16 [16, 32, 38, 128, 128], P('row', 'col'), may hold values from -0.15625 to 0.15625
- tile_rows: int32 [16, 32, 38], P('row', 'col'), may hold values from 0 to 31
- tile_cols: int32 [16, 32, 38], P('row', 'col'), may hold values from 0 to 15
- tile_counts: int32 [16, 32], P('row', 'col'), may hold values from 4 to 38, as said below
- out_grad: bfloat16 [65536, 128], P(('row', 'col')), may hold values from -6 to 6
Outputs:
- activated: bfloat16 [65536, 128], P(('row', 'col'))
- x_grad: bfloat16 [65536, 128], P(('row', 'col'))
- weight_grad: float32 [128, 128], replicated
- bias_grad: float32 [128], replicated
The draws below stay inside these ranges and needn't reach their ends.
Inputs may be any that keep to these rules, and one draw needn't show every extreme that they name: `tile_counts`: some grid cell has exactly 38 live slots in every draw.
All inputs are finite; a program needn't handle non-finite values.
Results may differ from the reference program's by a relative error of at most 0.024.
Values may be sent and summed in bfloat16 or wider, within the bound.
A program may use at most 64 MiB of HBM per device.

```python
import jax
import jax.numpy as jnp
from jax import lax

FIN = 128
HID = 128
BLK = 128
SLICE = 128
MAXT = 38
GROWS = 16
GCOLS = 32
NODES = 65536
RBLK = 32
PBLK = 16
N_ROW = 16
N_COL = 32


def draw_tile_counts(key, part):
    key = jax.random.fold_in(key, 7)
    first, second = jax.random.split(key)
    base = jax.random.randint(first, (N_ROW, N_COL), MAXT // 8, MAXT // 2 + 1)
    picked = jax.random.randint(second, (), 0, N_ROW * N_COL)
    flat = jnp.arange(N_ROW * N_COL, dtype=jnp.int32).reshape(N_ROW, N_COL)
    return jnp.where(flat == picked, MAXT, base).astype(jnp.int32)


def set_ends(values, rng, low, largest):
    longest = values.shape.index(max(values.shape))
    spots = []
    for shift in (0, 1):
        where = [jax.random.randint(jax.random.fold_in(rng, axis), (), 0, length) for axis, length in enumerate(values.shape)]
        where[longest] = (where[longest] + shift) % values.shape[longest]
        spots.append(tuple(where))
    return values.at[spots[0]].set(low).at[spots[1]].set(largest)


def level_of(own_key, extent, cuts, least, top_value):
    def one(position, shards_of):
        heights = jax.random.uniform(jax.random.fold_in(jax.random.fold_in(own_key, 6), position), (shards_of,), jnp.float32, least / len(cuts), top_value / len(cuts))
        return jnp.repeat(jnp.exp(heights), extent[position] // shards_of).reshape((-1,) + (1,) * (len(extent) - position - 1))

    loudness = one(*cuts[0])
    for cut in cuts[1:]:
        loudness = loudness * one(*cut)
    return loudness


def centred(own_key, shape, width, limit, pieces=(), kind=jnp.bfloat16):
    entries = jax.random.normal(own_key, shape, jnp.float32) * width
    if len(pieces) > 0:
        entries = level_of(own_key, shape, pieces, -0.22, 0.18) * entries
    return jnp.clip(entries, min=-limit, max=limit).astype(kind)


def setup_inputs(seed: int = 0) -> dict:
    keys = jax.random.split(jax.random.key(seed), 9)
    return {
        "features": centred(keys[0], (NODES, FIN), 1.0, 6.0, ((0, 512),)),
        "weight": centred(keys[1], (FIN, HID), FIN ** -0.5, 0.5),
        "bias": centred(keys[2], (HID,), 0.5, 3.0, (), jnp.float32),
        "tile_values": centred(keys[3], (GROWS, GCOLS, MAXT, BLK, BLK), (BLK * MAXT * N_COL // (3 * RBLK)) ** -0.5, 0.15625, ((0, 16), (1, 32))),
        "tile_rows": set_ends(jax.random.randint(keys[4], (GROWS, GCOLS, MAXT), 0, RBLK), jax.random.fold_in(keys[4], 1), 0, RBLK - 1).astype(jnp.int32),
        "tile_cols": set_ends(jax.random.randint(keys[5], (GROWS, GCOLS, MAXT), 0, PBLK), jax.random.fold_in(keys[5], 1), 0, PBLK - 1).astype(jnp.int32),
        "tile_counts": draw_tile_counts(jax.random.fold_in(keys[8], 71), 0),
        "out_grad": centred(keys[7], (NODES, HID), 1.0, 6.0, ((0, 512),)),
    }


def silu_slope(value):
    sig = jax.nn.sigmoid(value)
    return sig * (1.0 + value * (1.0 - sig))


def reference(features, weight, bias, tile_values, tile_rows, tile_cols, tile_counts, out_grad):
    proj = jnp.dot(features, weight, preferred_element_type=jnp.float32).astype(jnp.bfloat16)
    panels = proj.reshape(N_ROW, N_COL, SLICE, HID).transpose(1, 0, 2, 3).reshape(N_COL, PBLK, BLK, HID)
    slots = jnp.arange(MAXT, dtype=jnp.int32)

    def forward_cell(cell, total):
        rindex = cell // N_COL
        cindex = cell % N_COL
        tiles = tile_values[rindex, cindex].astype(jnp.float32)
        valid = (slots < tile_counts[rindex, cindex]).astype(jnp.float32)
        blocks = panels[cindex][tile_cols[rindex, cindex]].astype(jnp.float32)
        prod = jnp.einsum('tij,tjf->tif', tiles, blocks) * valid[:, None, None]
        added = jax.ops.segment_sum(prod, tile_rows[rindex, cindex], num_segments=RBLK)
        return total.at[rindex].add(added)

    sums = lax.fori_loop(0, N_ROW * N_COL, forward_cell, jnp.zeros((N_ROW, RBLK, BLK, HID), jnp.float32))
    pre = sums.reshape(NODES, HID) + bias.astype(jnp.float32)[None, :]
    activated = jax.nn.silu(pre).astype(jnp.bfloat16)
    grad = (out_grad.astype(jnp.float32) * silu_slope(pre)).astype(jnp.bfloat16)
    grad_blocks = grad.reshape(N_ROW, RBLK, BLK, HID)

    def backward_cell(cell, total):
        rindex = cell // N_COL
        cindex = cell % N_COL
        tiles = tile_values[rindex, cindex].astype(jnp.float32)
        valid = (slots < tile_counts[rindex, cindex]).astype(jnp.float32)
        blocks = grad_blocks[rindex][tile_rows[rindex, cindex]].astype(jnp.float32)
        prod = jnp.einsum('tji,tjf->tif', tiles, blocks) * valid[:, None, None]
        added = jax.ops.segment_sum(prod, tile_cols[rindex, cindex], num_segments=PBLK)
        return total.at[cindex].add(added)

    back = lax.fori_loop(0, N_ROW * N_COL, backward_cell, jnp.zeros((N_COL, PBLK, BLK, HID), jnp.float32))
    back_b = back.reshape(N_COL, N_ROW, SLICE, HID).transpose(1, 0, 2, 3).reshape(NODES, HID).astype(jnp.bfloat16)
    x_grad = jnp.dot(back_b, weight.T, preferred_element_type=jnp.float32).astype(jnp.bfloat16)
    weight_grad = jnp.dot(features.T, back_b, preferred_element_type=jnp.float32)
    bias_grad = jnp.sum(grad.astype(jnp.float32), axis=0)
    return (activated, x_grad, weight_grad, bias_grad)
```

```python
import jax
import jax.numpy as jnp
from jax import lax
from jax.experimental import pallas as pl
from jax.experimental.pallas import tpu as pltpu
from jax.sharding import PartitionSpec as P

MESH = pl.DeviceIdType.MESH
F32 = jnp.float32
BF16 = jnp.bfloat16
SIDE = 128
SLOTS = 38
NY, NZ, NCORE = 4, 16, 2
N_ROW, N_COL = 16, 32

CHIPS = ((2, 1), (2, 0), (1, 1), (3, 1), (1, 0), (3, 0), (0, 1))
PARENT = {2: 0, 6: 0, -2: 0, -6: 0, 1: 2, 3: 2, 4: 2, 5: 6, 7: 6, 8: 6, -1: -2, -3: -2, -4: -2, -5: -6, -7: -6}
CHILDREN = {p: [q for q in PARENT if PARENT[q] == p] for p in (0, 2, -2, 6, -6)}
REDUCE_ORDER = (8, 7, 5, -7, -5, 4, -4, 6, -6, 3, -3, 1, -1, 2, -2, 0)
GATHER_ORDER = (2, -2, 6, -6, 1, -1, 3, -3, 4, -4, 5, -5, 7, -7, 8)
ROUND_A = ((4, 0), (12, 0), (8, 0))
ROUND_B = ((0, 1), (1, 0), (15, 0), (2, 0), (1, 1), (15, 1), (2, 1))
ROW_PEERS = tuple((dy, dx, dk) for dy in range(4) for dx in range(2) for dk in range(2) if (dy, dx, dk) != (0, 0, 0))


def kernel(
    feat, weight, bias, tiles_hbm, rows, cols, counts, out_grad,
    act_out, xg_out, wg_out, bg_out,
    tiles, panel, partial, grads, table, tab,
    xs, xr, zs, zr, cs, cr, hs, hr, ws, wr, acc_a, wra, acc_b, wrb, fin,
    sem, p_s, p_r, f_s, f_r, xs_s, xs_r, zs_s, zs_r, g_s, g_r, gx_s, gx_r,
    c_s, c_r, h_s, h_r, w_s, w_r, a_s, a_r, b_s, b_r, e_s, e_r,
):
    r = lax.axis_index("row")
    c = lax.axis_index("col")
    core, xl, y = r % 2, (r // 2) % 2, r // 4
    z, xh = c // 2, c % 2

    def in_row(dy, dx, dk):
        xx = xl + dx - 2 * xl * dx
        kk = core + dk - 2 * core * dk
        return ((y + dy) % NY) * 4 + xx * 2 + kk

    def in_col(dz, dh):
        hh = xh + dh - 2 * xh * dh
        return ((z + dz + NZ) % NZ) * 2 + hh

    def send(src, dst, ss, rs, row, col):
        copy = pltpu.make_async_remote_copy(
            src_ref=src, dst_ref=dst, send_sem=ss, recv_sem=rs, device_id=(row, col), device_id_type=MESH
        )
        copy.start()
        started.append(copy)

    def landed(dst, rs):
        pltpu.make_async_remote_copy(
            src_ref=dst, dst_ref=dst, send_sem=rs, recv_sem=rs, device_id=(r, c), device_id_type=MESH
        ).wait_recv()

    started = []
    fetch = pltpu.make_async_copy(tiles_hbm, tiles, sem.at[0])
    fetch.start()

    barrier = pltpu.get_barrier_semaphore()
    greet = [(in_row(0, 0, 1), c)] + [(in_row(dy, dx, 0), c) for dy, dx in CHIPS]
    greet += [(r, in_col(0, 1))] + [(r, in_col(d, 0)) for d in (1, -1, 2, -2, 6, -6)]
    for row, col in greet:
        pl.semaphore_signal(barrier, inc=1, device_id=(row, col), device_id_type=MESH)

    lane = lax.broadcasted_iota(jnp.int32, (SIDE, SIDE), 1)
    sub = lax.broadcasted_iota(jnp.int32, (SIDE, SIDE), 0)
    live = sub < counts[0, 0]
    for k, ref in ((0, rows), (1, cols)):
        padded = jnp.concatenate([ref[...], jnp.zeros((1, SIDE - SLOTS), jnp.int32)], axis=1)
        along = jnp.broadcast_to(padded, (SIDE, SIDE))
        down = jnp.sum(jnp.where(lane == sub, along, 0), axis=1, keepdims=True)
        down = jnp.broadcast_to(down, (SIDE, SIDE))
        prev = jnp.max(jnp.where((down == along) & (sub < lane) & live, sub + 1, 0), axis=0, keepdims=True)
        last = jnp.max(jnp.where((down == lane) & live, sub + 1, 0), axis=0, keepdims=True)
        table[k : k + 1, :] = padded
        table[2 + k : 3 + k, :] = prev
        table[4 + k : 5 + k, :] = last
    table[6:8, :] = jnp.zeros((2, SIDE), jnp.int32)
    to_scalar = pltpu.make_async_copy(table, tab, sem.at[1])
    to_scalar.start()
    panel[r] = feat[...]
    partial[0] = jnp.zeros((SIDE, SIDE), F32)

    pl.semaphore_wait(barrier, len(greet))

    for k, (dy, dx) in enumerate(CHIPS):
        send(feat, panel.at[r], p_s.at[k], p_r.at[k], in_row(dy, dx, 0), c)
    send(feat, panel.at[r], p_s.at[7], p_r.at[7], in_row(0, 0, 1), c)
    for k in (6, 4, 5, 1, 2, 3, 0):
        dy, dx = CHIPS[k]
        p = in_row(4 - dy, dx, 0)
        landed(panel.at[p], p_r.at[k])
        send(panel.at[p], panel.at[p], f_s.at[k], f_r.at[k], in_row(0, 0, 1), c)
    landed(panel.at[in_row(0, 0, 1)], p_r.at[7])
    to_scalar.wait()
    fetch.wait()
    for k, (dy, dx) in enumerate(CHIPS):
        landed(panel.at[in_row(4 - dy, dx, 1)], f_r.at[k])

    def forward(t, carry):
        prod = jnp.dot(tiles[t], panel[tab[1, t]], preferred_element_type=F32)
        partial[t + 1] = prod + partial[tab[2, t]]
        return carry

    lax.fori_loop(0, SLOTS, forward, 0, unroll=True)

    for e in REDUCE_ORDER:
        b = in_col(-e, 1)
        xs[e % NZ] = partial[tab[4, b]].astype(BF16)
        send(xs.at[e % NZ], xr.at[e % NZ], xs_s.at[e % NZ], xs_r.at[e % NZ], r, in_col(0, 1))
    total = None
    for e in REDUCE_ORDER:
        i = e % NZ
        total = partial[tab[4, in_col(-e, 0)]]
        for q in CHILDREN.get(e, ()):
            landed(zr.at[q % NZ], zs_r.at[q % NZ])
            total += zr[q % NZ].astype(F32)
        landed(xr.at[i], xs_r.at[i])
        total += xr[i].astype(F32)
        if e != 0:
            zs[i] = total.astype(BF16)
            send(zs.at[i], zr.at[i], zs_s.at[i], zs_r.at[i], r, in_col(PARENT[e] - e, 0))

    agg = total.astype(BF16)
    pre = jnp.dot(agg, weight[...], preferred_element_type=F32) + bias[...]
    sig = 1.0 / (1.0 + jnp.exp(-pre))
    grad = (out_grad[...].astype(F32) * (sig * (1.0 + pre * (1.0 - sig)))).astype(BF16)
    grads[c] = grad.T

    for k in (6, -6):
        send(grads.at[c], grads.at[c], g_s.at[k % NZ], g_r.at[k % NZ], r, in_col(k, 0))
    send(grads.at[c], grads.at[c], gx_s.at[0], gx_r.at[0], r, in_col(0, 1))
    for k in (2, -2):
        send(grads.at[c], grads.at[c], g_s.at[k % NZ], g_r.at[k % NZ], r, in_col(k, 0))

    act_out[...] = (pre * sig).astype(BF16)
    wgrad = lax.dot_general(agg, grad, (((0,), (0,)), ((), ())), preferred_element_type=F32)
    bgrad = jnp.sum(grad.astype(F32).reshape(16, 8, SIDE), axis=0)
    ws[:, 0:8, :] = wgrad.reshape(N_ROW, 8, SIDE)
    ws[:, 8:16, :] = jnp.broadcast_to(bgrad[None], (N_ROW, 8, SIDE))
    for k, (dy, dx, dk) in enumerate(ROW_PEERS):
        to = in_row(dy, dx, dk)
        send(ws.at[to], wr.at[k], w_s.at[k], w_r.at[k], to, c)

    def take(d):
        i = d % NZ
        b = in_col(-d, 0)
        landed(grads.at[b], g_r.at[i])
        for q in CHILDREN.get(d, ()):
            send(grads.at[b], grads.at[b], g_s.at[q % NZ], g_r.at[q % NZ], r, in_col(q - d, 0))
        send(grads.at[b], grads.at[b], gx_s.at[i], gx_r.at[i], r, in_col(0, 1))

    for d in GATHER_ORDER[:4]:
        take(d)
    total = ws[r]
    for k in range(len(ROW_PEERS)):
        landed(wr.at[k], w_r.at[k])
        total += wr[k]
    acc_a[...] = total
    for k, (dz, dh) in enumerate(ROUND_A):
        send(acc_a, wra.at[k], a_s.at[k], a_r.at[k], r, in_col(dz, dh))
    for d in GATHER_ORDER[4:]:
        take(d)
    total = acc_a[...]
    for k in range(len(ROUND_A)):
        landed(wra.at[k], a_r.at[k])
        total += wra[k]
    acc_b[...] = total
    for k, (dz, dh) in enumerate(ROUND_B):
        send(acc_b, wrb.at[k], b_s.at[k], b_r.at[k], r, in_col(dz, dh))
    landed(grads.at[in_col(0, 1)], gx_r.at[0])
    for d in GATHER_ORDER:
        landed(grads.at[in_col(-d, 1)], gx_r.at[d % NZ])

    def backward(t, carry):
        prod = jnp.dot(grads[tab[0, t]], tiles[t], preferred_element_type=F32)
        partial[t + 1] = prod + partial[tab[3, t]]
        return carry

    lax.fori_loop(0, SLOTS, backward, 0, unroll=True)

    for k, (dy, dx) in enumerate(CHIPS + ((0, 0),)):
        cs[k] = partial[tab[5, in_row(dy, dx, 1)]].astype(BF16)
        send(cs.at[k], cr.at[k], c_s.at[k], c_r.at[k], in_row(0, 0, 1), c)
    for k, (dy, dx) in enumerate(CHIPS):
        landed(cr.at[k], c_r.at[k])
        hs[k] = (partial[tab[5, in_row(dy, dx, 0)]] + cr[k].astype(F32)).astype(BF16)
        send(hs.at[k], hr.at[k], h_s.at[k], h_r.at[k], in_row(dy, dx, 0), c)

    total = acc_b[...]
    for k in range(len(ROUND_B)):
        landed(wrb.at[k], b_r.at[k])
        total += wrb[k]
    fin[r] = total[0:8]
    bg_out[...] = jnp.sum(total[8:16], axis=0, keepdims=True)
    for k, (dy, dx, dk) in enumerate(ROW_PEERS):
        send(fin.at[r], fin.at[r], e_s.at[k], e_r.at[k], in_row(dy, dx, dk), c)

    landed(cr.at[7], c_r.at[7])
    total = partial[tab[5, r]] + cr[7].astype(F32)
    for k in (6, 4, 5, 1, 2, 3, 0):
        landed(hr.at[k], h_r.at[k])
        total += hr[k].astype(F32)
    back = total.astype(BF16)
    xg_out[...] = lax.dot_general(
        back, weight[...], (((0,), (1,)), ((), ())), preferred_element_type=F32
    ).astype(BF16)
    for k, (dy, dx, dk) in enumerate(ROW_PEERS):
        landed(fin.at[in_row(4 - dy, dx, dk)], e_r.at[k])
    wg_out[...] = fin[...].reshape(SIDE, SIDE)
    for copy in started:
        copy.wait_send()


def on_device(features, weight, bias, tile_values, tile_rows, tile_cols, tile_counts, out_grad):
    vmem = pl.BlockSpec(memory_space=pltpu.VMEM)
    dma = pltpu.SemaphoreType.DMA
    block = (SIDE, SIDE)
    act, xg, wg, bg = pl.pallas_call(
        kernel,
        name="gcn",
        out_shape=(
            jax.ShapeDtypeStruct(block, BF16),
            jax.ShapeDtypeStruct(block, BF16),
            jax.ShapeDtypeStruct(block, F32),
            jax.ShapeDtypeStruct((1, SIDE), F32),
        ),
        in_specs=[
            vmem, vmem, vmem, pl.BlockSpec(memory_space=pl.ANY), vmem, vmem,
            pl.BlockSpec(memory_space=pltpu.SMEM), vmem,
        ],
        out_specs=(vmem,) * 4,
        scratch_shapes=[
            pltpu.VMEM((SLOTS,) + block, BF16),
            pltpu.VMEM((N_ROW,) + block, BF16),
            pltpu.VMEM((SLOTS + 1,) + block, F32),
            pltpu.VMEM((N_COL,) + block, BF16),
            pltpu.VMEM((8, SIDE), jnp.int32),
            pltpu.SMEM((8, SIDE), jnp.int32),
            pltpu.VMEM((NZ,) + block, BF16),
            pltpu.VMEM((NZ,) + block, BF16),
            pltpu.VMEM((NZ,) + block, BF16),
            pltpu.VMEM((NZ,) + block, BF16),
            pltpu.VMEM((8,) + block, BF16),
            pltpu.VMEM((8,) + block, BF16),
            pltpu.VMEM((7,) + block, BF16),
            pltpu.VMEM((7,) + block, BF16),
            pltpu.VMEM((N_ROW, 16, SIDE), F32),
            pltpu.VMEM((15, 16, SIDE), F32),
            pltpu.VMEM((16, SIDE), F32),
            pltpu.VMEM((3, 16, SIDE), F32),
            pltpu.VMEM((16, SIDE), F32),
            pltpu.VMEM((7, 16, SIDE), F32),
            pltpu.VMEM((N_ROW, 8, SIDE), F32),
            dma((2,)),
            dma((8,)), dma((8,)), dma((7,)), dma((7,)),
            dma((NZ,)), dma((NZ,)), dma((NZ,)), dma((NZ,)),
            dma((NZ,)), dma((NZ,)), dma((NZ,)), dma((NZ,)),
            dma((8,)), dma((8,)), dma((7,)), dma((7,)),
            dma((15,)), dma((15,)), dma((3,)), dma((3,)), dma((7,)), dma((7,)), dma((15,)), dma((15,)),
        ],
        compiler_params=pltpu.CompilerParams(
            collective_id=0, has_side_effects=True, vmem_limit_bytes=32 << 20
        ),
    )(
        features, weight, bias.reshape(1, SIDE), tile_values[0, 0],
        tile_rows[0], tile_cols[0], tile_counts, out_grad,
    )
    return act, xg, wg, bg.reshape(SIDE)


def solution(mesh):
    return jax.shard_map(
        on_device,
        mesh=mesh,
        in_specs=(
            P(("row", "col"), None),
            P(),
            P(),
            P("row", "col", None, None, None),
            P("row", "col", None),
            P("row", "col", None),
            P("row", "col"),
            P(("row", "col"), None),
        ),
        out_specs=(P(("row", "col"), None), P(("row", "col"), None), P(), P()),
        check_vma=False,
    )
```

```python
import jax
import jax.numpy as jnp
from jax import lax
from jax.experimental import pallas as pl
from jax.experimental.pallas import tpu as pltpu
from jax.sharding import PartitionSpec as P

MESH = pl.DeviceIdType.MESH
F32 = jnp.float32
BF16 = jnp.bfloat16
SIDE = 128
SLOTS = 38
NY, NZ, NCORE = 4, 16, 2
N_ROW, N_COL = 16, 32

CHIPS = ((2, 1), (2, 0), (1, 1), (3, 1), (1, 0), (3, 0), (0, 1))
SUM_PARENT = {
    -7: -6, -6: -5, -5: 0, -4: -5, -3: -2, -2: 0, -1: 0, 1: 0, 2: 0, 3: 2, 4: 5, 5: 0, 6: 5, 7: 6, 8: 5,
}
SUM_BOTH = (-7, -6, -3, 3, 6, 7)
SUM_PLAN = (
    ("z2", 7), ("x", 8), ("z2", -7), ("z1", -7), ("x", -4), ("z2", -3), ("z1", 7), ("x", 4), ("x", 0), ("x", 1),
    ("z2", 3), ("x", -1), ("z1", -3), ("z1", 3), ("z2", 6), ("z2", -6), ("z1", 6), ("z1", -6), ("z1", 8), ("x", 2),
    ("x", -2), ("z1", -4), ("z1", 4), ("x", 5), ("x", -5), ("z1", 1), ("z1", -1), ("z1", 2), ("z1", -2), ("z1", 5),
    ("z1", -5),
)
GET_PARENT = {
    -7: -6, -6: 0, -5: -6, -4: -3, -3: -2, -2: 0, -1: -2, 1: 2, 2: 0, 3: 2, 4: 3, 5: 6, 6: 0, 7: 6, 8: 7,
}
GET_BOTH = (-7, -4, 1, 4, 7)
GET_CROSS = (-3, 3, 5, 8)
GET_FIRST = (("z1", 6), ("z1", -6), ("z1", 2), ("z1", -2), ("x", 0))
GET_NEXT = (
    ("dg", 3), ("z1", 3), ("x", 2), ("z1", 1), ("z1", -3), ("x", -2), ("dg", -3), ("z1", -1),
)
GET_LAST = (
    ("x", 6), ("z1", 7), ("dg", 5), ("z1", 5), ("z1", -7), ("x", -6), ("z1", -5), ("z2", 1), ("z1", 4), ("z1", -4),
    ("z2", 4), ("x", -1), ("dg", 8), ("z1", 8), ("z2", -4), ("x", -5), ("z2", 7), ("z2", -7),
)
ROUND_A = ((4, 0), (12, 0), (8, 0))
ROUND_B = ((0, 1), (1, 0), (15, 0), (2, 0), (1, 1), (15, 1), (2, 1))
ROW_PEERS = tuple((dy, dx, dk) for dy in range(4) for dx in range(2) for dk in range(2) if (dy, dx, dk) != (0, 0, 0))


def kernel(
    feat_hbm, weight_hbm, bias_hbm, tiles_hbm, rows_hbm, cols_hbm, counts_hbm, out_grad_hbm,
    act_out, back_out, wg_out, bg_out,
    weight, bias, rows, cols, counts, out_grad, tiles, panel, partial, grads, table, tab,
    xs, xr, z1s, z1r, z2s, z2r, cs, cr, hs, hr, ws, wr, acc_a, wra, acc_b, wrb, fin,
    sem, ring, p_s, p_r, f_s, f_r, xs_s, xs_r, z1_s, z1_r, z2_s, z2_r,
    g1_s, g1_r, g2_s, g2_r, gd_s, gd_r, gx_s, gx_r,
    c_s, c_r, h_s, h_r, w_s, w_r, a_s, a_r, b_s, b_r, e_s, e_r,
):
    r = lax.axis_index("row")
    c = lax.axis_index("col")
    core, xl, y = r % 2, (r // 2) % 2, r // 4
    z, xh = c // 2, c % 2

    def in_row(dy, dx, dk):
        xx = xl + dx - 2 * xl * dx
        kk = core + dk - 2 * core * dk
        return ((y + dy) % NY) * 4 + xx * 2 + kk

    def in_col(dz, dh):
        hh = xh + dh - 2 * xh * dh
        return ((z + dz + NZ) % NZ) * 2 + hh

    def send(src, dst, ss, rs, row, col):
        copy = pltpu.make_async_remote_copy(
            src_ref=src, dst_ref=dst, send_sem=ss, recv_sem=rs, device_id=(row, col), device_id_type=MESH
        )
        copy.start()
        started.append(copy)

    def landed(dst, rs):
        pltpu.make_async_remote_copy(
            src_ref=dst, dst_ref=dst, send_sem=rs, recv_sem=rs, device_id=(r, c), device_id_type=MESH
        ).wait_recv()

    started = []
    g_s = {"z1": g1_s, "z2": g2_s, "dg": gd_s, "x": gx_s}
    g_r = {"z1": g1_r, "z2": g2_r, "dg": gd_r, "x": gx_r}
    fetch = [
        pltpu.make_async_copy(src, dst, sem.at[k])
        for k, (src, dst) in enumerate(
            (
                (feat_hbm, panel.at[r]), (rows_hbm, rows), (cols_hbm, cols), (counts_hbm, counts),
                (tiles_hbm, tiles), (weight_hbm, weight), (bias_hbm, bias), (out_grad_hbm, out_grad),
            )
        )
    ]
    for copy in fetch:
        copy.start()

    barrier = pltpu.get_barrier_semaphore()
    greet = [(in_row(0, 0, 1), c)] + [(in_row(dy, dx, 0), c) for dy, dx in CHIPS]
    greet += [(r, in_col(0, 1))] + [(r, in_col(d, 0)) for d in (1, -1, 2, -2, 3, -3)]
    for row, col in greet:
        pl.semaphore_signal(barrier, inc=1, device_id=(row, col), device_id_type=MESH)

    for k in (1, 2, 3):
        fetch[k].wait()
    lane = lax.broadcasted_iota(jnp.int32, (SIDE, SIDE), 1)
    sub = lax.broadcasted_iota(jnp.int32, (SIDE, SIDE), 0)
    live = sub < counts[0, 0]
    for k, ref in ((0, rows), (1, cols)):
        padded = jnp.concatenate([ref[...], jnp.zeros((1, SIDE - SLOTS), jnp.int32)], axis=1)
        along = jnp.broadcast_to(padded, (SIDE, SIDE))
        down = jnp.sum(jnp.where(lane == sub, along, 0), axis=1, keepdims=True)
        down = jnp.broadcast_to(down, (SIDE, SIDE))
        prev = jnp.max(jnp.where((down == along) & (sub < lane) & live, sub + 1, 0), axis=0, keepdims=True)
        last = jnp.max(jnp.where((down == lane) & live, sub + 1, 0), axis=0, keepdims=True)
        table[k : k + 1, :] = padded
        table[2 + k : 3 + k, :] = prev
        table[4 + k : 5 + k, :] = last
    table[6:8, :] = jnp.zeros((2, SIDE), jnp.int32)
    to_scalar = pltpu.make_async_copy(table, tab, sem.at[8])
    to_scalar.start()
    partial[0] = jnp.zeros((SIDE, SIDE), F32)

    fetch[0].wait()
    pl.semaphore_wait(barrier, len(greet))

    for d in (3, -3):
        pl.semaphore_signal(ring, inc=1, device_id=(r, in_col(d, 0)), device_id_type=MESH)

    for k, (dy, dx) in enumerate(CHIPS):
        send(panel.at[r], panel.at[r], p_s.at[k], p_r.at[k], in_row(dy, dx, 0), c)
    send(panel.at[r], panel.at[r], p_s.at[7], p_r.at[7], in_row(0, 0, 1), c)
    for k in (6, 4, 5, 1, 2, 3, 0):
        dy, dx = CHIPS[k]
        p = in_row(4 - dy, dx, 0)
        landed(panel.at[p], p_r.at[k])
        send(panel.at[p], panel.at[p], f_s.at[k], f_r.at[k], in_row(0, 0, 1), c)
    landed(panel.at[in_row(0, 0, 1)], p_r.at[7])
    to_scalar.wait()
    fetch[4].wait()
    for k, (dy, dx) in enumerate(CHIPS):
        landed(panel.at[in_row(4 - dy, dx, 1)], f_r.at[k])

    def forward(t, carry):
        prod = jnp.dot(tiles[t], panel[tab[1, t]], preferred_element_type=F32)
        partial[t + 1] = prod + partial[tab[2, t]]
        return carry

    lax.fori_loop(0, SLOTS, forward, 0, unroll=True)

    pl.semaphore_wait(ring, 2)

    def collect(e, kind):
        i = e % NZ
        own = in_col(-e, 0) if kind == "z1" else in_col(-e, 1)
        value = partial[tab[4, own]]
        for q in SUM_PARENT:
            if SUM_PARENT[q] == e and (kind == "z1" or q in SUM_BOTH):
                buf, got = (z1r, z1_r) if kind == "z1" else (z2r, z2_r)
                landed(buf.at[q % NZ], got.at[q % NZ])
                value += buf[q % NZ].astype(F32)
        if kind == "z1" and e not in SUM_BOTH:
            landed(xr.at[i], xs_r.at[i])
            value += xr[i].astype(F32)
        return value

    for kind, e in SUM_PLAN:
        i = e % NZ
        value = collect(e, kind).astype(BF16)
        if kind == "x":
            xs[i] = value
            send(xs.at[i], xr.at[i], xs_s.at[i], xs_r.at[i], r, in_col(0, 1))
        elif kind == "z1":
            z1s[i] = value
            send(z1s.at[i], z1r.at[i], z1_s.at[i], z1_r.at[i], r, in_col(SUM_PARENT[e] - e, 0))
        else:
            z2s[i] = value
            send(z2s.at[i], z2r.at[i], z2_s.at[i], z2_r.at[i], r, in_col(SUM_PARENT[e] - e, 0))
    total = collect(0, "z1")

    for k in (5, 6, 7):
        fetch[k].wait()
    agg = total.astype(BF16)
    pre = jnp.dot(agg, weight[...], preferred_element_type=F32) + bias[...]
    sig = 1.0 / (1.0 + jnp.exp(-pre))
    grad = (out_grad[...].astype(F32) * (sig * (1.0 + pre * (1.0 - sig)))).astype(BF16)
    grads[c] = grad.T

    got = set()

    def have(kind, d):
        if (kind, d) not in got:
            got.add((kind, d))
            landed(grads.at[in_col(-d, 0 if kind == "z1" else 1)], g_r[kind].at[d % NZ])

    def second(d):
        return "z2" if d in GET_BOTH else "dg" if d in GET_CROSS else "x"

    def follow(plan):
        for kind, d in plan:
            p = d if kind == "x" else GET_PARENT[d]
            if kind == "z2":
                have(second(p), p)
            elif p != 0:
                have("z1", p)
            block = grads.at[in_col(-p, 1 if kind == "z2" else 0)]
            to = in_col(d - p, 1 if kind in ("x", "dg") else 0)
            send(block, block, g_s[kind].at[d % NZ], g_r[kind].at[d % NZ], r, to)

    follow(GET_FIRST)
    act_out[...] = (pre * sig).astype(BF16)
    wgrad = lax.dot_general(agg, grad, (((0,), (0,)), ((), ())), preferred_element_type=F32)
    bgrad = jnp.sum(grad.astype(F32).reshape(16, 8, SIDE), axis=0)
    ws[:, 0:8, :] = wgrad.reshape(N_ROW, 8, SIDE)
    ws[:, 8:16, :] = jnp.broadcast_to(bgrad[None], (N_ROW, 8, SIDE))
    for k, (dy, dx, dk) in enumerate(ROW_PEERS):
        to = in_row(dy, dx, dk)
        send(ws.at[to], wr.at[k], w_s.at[k], w_r.at[k], to, c)

    follow(GET_NEXT)
    total = ws[r]
    for k in range(len(ROW_PEERS)):
        landed(wr.at[k], w_r.at[k])
        total += wr[k]
    acc_a[...] = total
    for k, (dz, dh) in enumerate(ROUND_A):
        send(acc_a, wra.at[k], a_s.at[k], a_r.at[k], r, in_col(dz, dh))
    follow(GET_LAST)
    total = acc_a[...]
    for k in range(len(ROUND_A)):
        landed(wra.at[k], a_r.at[k])
        total += wra[k]
    acc_b[...] = total
    for k, (dz, dh) in enumerate(ROUND_B):
        send(acc_b, wrb.at[k], b_s.at[k], b_r.at[k], r, in_col(dz, dh))
    have("x", 0)
    for d in GET_PARENT:
        have("z1", d)
        have(second(d), d)

    def backward(t, carry):
        prod = jnp.dot(grads[tab[0, t]], tiles[t], preferred_element_type=F32)
        partial[t + 1] = prod + partial[tab[3, t]]
        return carry

    lax.fori_loop(0, SLOTS, backward, 0, unroll=True)

    for k, (dy, dx) in enumerate(CHIPS + ((0, 0),)):
        cs[k] = partial[tab[5, in_row(dy, dx, 1)]].astype(BF16)
        send(cs.at[k], cr.at[k], c_s.at[k], c_r.at[k], in_row(0, 0, 1), c)
    for k, (dy, dx) in enumerate(CHIPS):
        landed(cr.at[k], c_r.at[k])
        hs[k] = (partial[tab[5, in_row(dy, dx, 0)]] + cr[k].astype(F32)).astype(BF16)
        send(hs.at[k], hr.at[k], h_s.at[k], h_r.at[k], in_row(dy, dx, 0), c)

    total = acc_b[...]
    for k in range(len(ROUND_B)):
        landed(wrb.at[k], b_r.at[k])
        total += wrb[k]
    fin[r] = total[0:8]
    bg_out[...] = jnp.sum(total[8:16], axis=0, keepdims=True)
    for k, (dy, dx, dk) in enumerate(ROW_PEERS):
        send(fin.at[r], fin.at[r], e_s.at[k], e_r.at[k], in_row(dy, dx, dk), c)

    landed(cr.at[7], c_r.at[7])
    total = partial[tab[5, r]] + cr[7].astype(F32)
    for k in (6, 4, 5, 1, 2, 3, 0):
        landed(hr.at[k], h_r.at[k])
        total += hr[k].astype(F32)
    back_out[...] = total.astype(BF16)
    for k, (dy, dx, dk) in enumerate(ROW_PEERS):
        landed(fin.at[in_row(4 - dy, dx, dk)], e_r.at[k])
    wg_out[...] = fin[...].reshape(SIDE, SIDE)
    for copy in started:
        copy.wait_send()


def finish(act, back, weight, wg, bg, act_out, xg_out, wg_out, bg_out):
    act_out[...] = act[...]
    xg_out[...] = lax.dot_general(
        back[...], weight[...], (((0,), (1,)), ((), ())), preferred_element_type=F32
    ).astype(BF16)
    wg_out[...] = wg[...]
    bg_out[...] = bg[...]


def on_device(features, weight, bias, tile_values, tile_rows, tile_cols, tile_counts, out_grad):
    vmem = pl.BlockSpec(memory_space=pltpu.VMEM)
    dma = pltpu.SemaphoreType.DMA
    block = (SIDE, SIDE)
    hbm = pl.BlockSpec(memory_space=pltpu.HBM)
    act, back, wg, bg = pl.pallas_call(
        kernel,
        name="gcn",
        out_shape=(
            jax.ShapeDtypeStruct(block, BF16),
            jax.ShapeDtypeStruct(block, BF16),
            jax.ShapeDtypeStruct(block, F32),
            jax.ShapeDtypeStruct((1, SIDE), F32),
        ),
        in_specs=[hbm] * 8,
        out_specs=(vmem,) * 4,
        scratch_shapes=[
            pltpu.VMEM(block, BF16),
            pltpu.VMEM((1, SIDE), F32),
            pltpu.VMEM((1, SLOTS), jnp.int32),
            pltpu.VMEM((1, SLOTS), jnp.int32),
            pltpu.SMEM((1, 1), jnp.int32),
            pltpu.VMEM(block, BF16),
            pltpu.VMEM((SLOTS,) + block, BF16),
            pltpu.VMEM((N_ROW,) + block, BF16),
            pltpu.VMEM((SLOTS + 1,) + block, F32),
            pltpu.VMEM((N_COL,) + block, BF16),
            pltpu.VMEM((8, SIDE), jnp.int32),
            pltpu.SMEM((8, SIDE), jnp.int32),
            *[pltpu.VMEM((NZ,) + block, BF16)] * 6,
            pltpu.VMEM((8,) + block, BF16),
            pltpu.VMEM((8,) + block, BF16),
            pltpu.VMEM((7,) + block, BF16),
            pltpu.VMEM((7,) + block, BF16),
            pltpu.VMEM((N_ROW, 16, SIDE), F32),
            pltpu.VMEM((15, 16, SIDE), F32),
            pltpu.VMEM((16, SIDE), F32),
            pltpu.VMEM((3, 16, SIDE), F32),
            pltpu.VMEM((16, SIDE), F32),
            pltpu.VMEM((7, 16, SIDE), F32),
            pltpu.VMEM((N_ROW, 8, SIDE), F32),
            dma((9,)),
            pltpu.SemaphoreType.REGULAR,
            dma((8,)), dma((8,)), dma((7,)), dma((7,)),
            *[dma((NZ,))] * 14,
            dma((8,)), dma((8,)), dma((7,)), dma((7,)),
            dma((15,)), dma((15,)), dma((3,)), dma((3,)), dma((7,)), dma((7,)), dma((15,)), dma((15,)),
        ],
        compiler_params=pltpu.CompilerParams(
            collective_id=0, has_side_effects=True, vmem_limit_bytes=60 << 20
        ),
    )(
        features, weight, bias.reshape(1, SIDE), tile_values[0, 0],
        tile_rows[0], tile_cols[0], tile_counts, out_grad,
    )
    act, xg, wg, bg = pl.pallas_call(
        finish,
        name="finish",
        out_shape=(
            jax.ShapeDtypeStruct(block, BF16),
            jax.ShapeDtypeStruct(block, BF16),
            jax.ShapeDtypeStruct(block, F32),
            jax.ShapeDtypeStruct((1, SIDE), F32),
        ),
        in_specs=[vmem] * 5,
        out_specs=(vmem,) * 4,
    )(act, back, weight, wg, bg)
    return act, xg, wg, bg.reshape(SIDE)


def solution(mesh):
    return jax.shard_map(
        on_device,
        mesh=mesh,
        in_specs=(
            P(("row", "col"), None),
            P(),
            P(),
            P("row", "col", None, None, None),
            P("row", "col", None),
            P("row", "col", None),
            P("row", "col"),
            P(("row", "col"), None),
        ),
        out_specs=(P(("row", "col"), None), P(("row", "col"), None), P(), P()),
        check_vma=False,
    )
```

```python
import jax
import jax.numpy as jnp
from jax import lax
from jax.experimental import pallas as pl
from jax.experimental.pallas import tpu as pltpu
from jax.sharding import PartitionSpec as P

MESH = pl.DeviceIdType.MESH
F32 = jnp.float32
BF16 = jnp.bfloat16
SIDE = 128
SLOTS = 38
NY, NZ, NCORE = 4, 16, 2
N_ROW, N_COL = 16, 32

CHIPS = ((2, 1), (2, 0), (1, 1), (3, 1), (1, 0), (3, 0), (0, 1))
SUM_PARENT = {-7: -6, -6: 0, -5: -6, -4: -3, -3: -1, -2: -1, -1: 0, 1: 0, 2: 3, 3: 1, 4: 3, 5: 6, 6: 0, 7: 6, 8: 6}
SUM_BOTH = (-5, -4, 2, 3, 4, 5)
SUM_CROSS = (-3, 7)
SUM_PLAN = (('z2', -5), ('z2', 2), ('x', 8), ('z1', -4), ('z1', 4), ('z2', 5), ('x', -7), ('dg', 7), ('z2', 4), ('z1', 7), ('x', -2), ('z1', 5), ('z2', -4), ('z1', -5), ('z1', 2), ('x', 0), ('x', -1), ('x', -6), ('z1', 8), ('z1', -3), ('z1', -7), ('x', 6), ('z2', 3), ('z1', -2), ('dg', -3), ('z1', 3), ('z1', -6), ('z1', 6), ('x', 1), ('z1', -1), ('z1', 1))
GET_PARENT = {
    -7: -6, -6: 0, -5: -6, -4: -3, -3: -2, -2: 0, -1: -2, 1: 2, 2: 0, 3: 2, 4: 3, 5: 6, 6: 0, 7: 6, 8: 7,
}
GET_BOTH = (-7, -4, 1, 4, 7)
GET_CROSS = (-3, 3, 5, 8)
GET_FIRST = (("z1", 6), ("z1", -6), ("z1", 2), ("z1", -2), ("x", 0))
GET_NEXT = (
    ("dg", 3), ("z1", 3), ("x", 2), ("z1", 1), ("z1", -3), ("x", -2), ("dg", -3), ("z1", -1),
)
GET_LAST = (
    ("x", 6), ("z1", 7), ("dg", 5), ("z1", 5), ("z1", -7), ("x", -6), ("z1", -5), ("z2", 1), ("z1", 4), ("z1", -4),
    ("z2", 4), ("x", -1), ("dg", 8), ("z1", 8), ("z2", -4), ("x", -5), ("z2", 7), ("z2", -7),
)
ROUND_A = ((4, 0), (12, 0), (8, 0))
ROUND_B = ((0, 1), (1, 0), (15, 0), (2, 0), (1, 1), (15, 1), (2, 1))
ROW_PEERS = tuple((dy, dx, dk) for dy in range(4) for dx in range(2) for dk in range(2) if (dy, dx, dk) != (0, 0, 0))


def kernel(
    feat_hbm, weight_hbm, bias_hbm, tiles_hbm, rows_hbm, cols_hbm, counts_hbm, out_grad_hbm,
    act_out, xg_out, wg_out, bg_out,
    weight, bias, rows, cols, counts, out_grad, tiles, panel, partial, grads, table, tab,
    xs, xr, z1s, z1r, z2s, z2r, dgr, cs, cr, hs, hr, ws, wr, acc_a, wra, acc_b, wrb, fin,
    sem, ring, p_s, p_r, f_s, f_r, xs_s, xs_r, z1_s, z1_r, z2_s, z2_r, dg_s, dg_r,
    g1_s, g1_r, g2_s, g2_r, gd_s, gd_r, gx_s, gx_r,
    c_s, c_r, h_s, h_r, w_s, w_r, a_s, a_r, b_s, b_r, e_s, e_r,
):
    r = lax.axis_index("row")
    c = lax.axis_index("col")
    core, xl, y = r % 2, (r // 2) % 2, r // 4
    z, xh = c // 2, c % 2

    def in_row(dy, dx, dk):
        xx = xl + dx - 2 * xl * dx
        kk = core + dk - 2 * core * dk
        return ((y + dy) % NY) * 4 + xx * 2 + kk

    def in_col(dz, dh):
        hh = xh + dh - 2 * xh * dh
        return ((z + dz + NZ) % NZ) * 2 + hh

    def send(src, dst, ss, rs, row, col):
        copy = pltpu.make_async_remote_copy(
            src_ref=src, dst_ref=dst, send_sem=ss, recv_sem=rs, device_id=(row, col), device_id_type=MESH
        )
        copy.start()
        started.append(copy)

    def landed(dst, rs):
        pltpu.make_async_remote_copy(
            src_ref=dst, dst_ref=dst, send_sem=rs, recv_sem=rs, device_id=(r, c), device_id_type=MESH
        ).wait_recv()

    started = []
    g_s = {"z1": g1_s, "z2": g2_s, "dg": gd_s, "x": gx_s}
    g_r = {"z1": g1_r, "z2": g2_r, "dg": gd_r, "x": gx_r}
    barrier = pltpu.get_barrier_semaphore()
    greet = [(in_row(dy, dx, 0), c) for dy, dx in CHIPS[:1]] + [(r, in_col(d, 0)) for d in (3, -3, 2, -2)]
    greet += [(r, in_col(0, 1))] + [(in_row(dy, dx, 0), c) for dy, dx in CHIPS[1:]]
    greet += [(r, in_col(d, 0)) for d in (1, -1)] + [(in_row(0, 0, 1), c)]
    for row, col in greet:
        pl.semaphore_signal(barrier, inc=1, device_id=(row, col), device_id_type=MESH)

    fetch = [
        pltpu.make_async_copy(src, dst, sem.at[k])
        for k, (src, dst) in enumerate(
            (
                (feat_hbm, panel.at[r]), (rows_hbm, rows), (cols_hbm, cols), (counts_hbm, counts),
                (tiles_hbm, tiles), (weight_hbm, weight), (bias_hbm, bias), (out_grad_hbm, out_grad),
            )
        )
    ]
    for copy in fetch:
        copy.start()

    fetch[0].wait()
    pl.semaphore_wait(barrier, len(greet))

    for dz, dh in ((3, 0), (-3, 0), (0, 1)):
        pl.semaphore_signal(ring, inc=1, device_id=(r, in_col(dz, dh)), device_id_type=MESH)

    for k, (dy, dx) in enumerate(CHIPS):
        send(panel.at[r], panel.at[r], p_s.at[k], p_r.at[k], in_row(dy, dx, 0), c)
    send(panel.at[r], panel.at[r], p_s.at[7], p_r.at[7], in_row(0, 0, 1), c)
    for k in (1, 2, 3):
        fetch[k].wait()
    lane = lax.broadcasted_iota(jnp.int32, (SIDE, SIDE), 1)
    sub = lax.broadcasted_iota(jnp.int32, (SIDE, SIDE), 0)
    live = sub < counts[0, 0]
    for k, ref in ((0, rows), (1, cols)):
        padded = jnp.concatenate([ref[...], jnp.zeros((1, SIDE - SLOTS), jnp.int32)], axis=1)
        along = jnp.broadcast_to(padded, (SIDE, SIDE))
        down = jnp.sum(jnp.where(lane == sub, along, 0), axis=1, keepdims=True)
        down = jnp.broadcast_to(down, (SIDE, SIDE))
        prev = jnp.max(jnp.where((down == along) & (sub < lane) & live, sub + 1, 0), axis=0, keepdims=True)
        last = jnp.max(jnp.where((down == lane) & live, sub + 1, 0), axis=0, keepdims=True)
        table[k : k + 1, :] = padded
        table[2 + k : 3 + k, :] = prev
        table[4 + k : 5 + k, :] = last
    table[6:8, :] = jnp.zeros((2, SIDE), jnp.int32)
    to_scalar = pltpu.make_async_copy(table, tab, sem.at[8])
    to_scalar.start()
    partial[0] = jnp.zeros((SIDE, SIDE), F32)


    for k in (6, 4, 5, 1, 2, 3, 0):
        dy, dx = CHIPS[k]
        p = in_row(4 - dy, dx, 0)
        landed(panel.at[p], p_r.at[k])
        send(panel.at[p], panel.at[p], f_s.at[k], f_r.at[k], in_row(0, 0, 1), c)
    landed(panel.at[in_row(0, 0, 1)], p_r.at[7])
    to_scalar.wait()
    fetch[4].wait()
    for k, (dy, dx) in enumerate(CHIPS):
        landed(panel.at[in_row(4 - dy, dx, 1)], f_r.at[k])

    def forward(t, carry):
        prod = jnp.dot(tiles[t], panel[tab[1, t]], preferred_element_type=F32)
        partial[t + 1] = prod + partial[tab[2, t]]
        return carry

    lax.fori_loop(0, SLOTS, forward, 0, unroll=True)

    pl.semaphore_wait(ring, 3)

    def collect(e, kind):
        i = e % NZ
        own = in_col(-e, 0) if kind == "z1" else in_col(-e, 1)
        value = partial[tab[4, own]]
        for q in SUM_PARENT:
            if SUM_PARENT[q] == e and (kind == "z1" or q in SUM_BOTH):
                buf, got = (z1r, z1_r) if kind == "z1" else (z2r, z2_r)
                landed(buf.at[q % NZ], got.at[q % NZ])
                value += buf[q % NZ].astype(F32)
            if SUM_PARENT[q] == e and kind == "z1" and q in SUM_CROSS:
                landed(dgr.at[q % NZ], dg_r.at[q % NZ])
                value += dgr[q % NZ].astype(F32)
        if kind == "z1" and e not in SUM_BOTH + SUM_CROSS:
            landed(xr.at[i], xs_r.at[i])
            value += xr[i].astype(F32)
        return value

    for kind, e in SUM_PLAN:
        i = e % NZ
        value = collect(e, kind).astype(BF16)
        if kind == "x":
            xs[i] = value
            send(xs.at[i], xr.at[i], xs_s.at[i], xs_r.at[i], r, in_col(0, 1))
        elif kind == "z1":
            z1s[i] = value
            send(z1s.at[i], z1r.at[i], z1_s.at[i], z1_r.at[i], r, in_col(SUM_PARENT[e] - e, 0))
        elif kind == "dg":
            z2s[i] = value
            send(z2s.at[i], dgr.at[i], dg_s.at[i], dg_r.at[i], r, in_col(SUM_PARENT[e] - e, 1))
        else:
            z2s[i] = value
            send(z2s.at[i], z2r.at[i], z2_s.at[i], z2_r.at[i], r, in_col(SUM_PARENT[e] - e, 0))
    total = collect(0, "z1")

    for k in (5, 6, 7):
        fetch[k].wait()
    agg = total.astype(BF16)
    pre = jnp.dot(agg, weight[...], preferred_element_type=F32) + bias[...]
    sig = 1.0 / (1.0 + jnp.exp(-pre))
    grad = (out_grad[...].astype(F32) * (sig * (1.0 + pre * (1.0 - sig)))).astype(BF16)
    grads[c] = grad.T

    got = set()

    def have(kind, d):
        if (kind, d) not in got:
            got.add((kind, d))
            landed(grads.at[in_col(-d, 0 if kind == "z1" else 1)], g_r[kind].at[d % NZ])

    def second(d):
        return "z2" if d in GET_BOTH else "dg" if d in GET_CROSS else "x"

    def follow(plan):
        for kind, d in plan:
            p = d if kind == "x" else GET_PARENT[d]
            if kind == "z2":
                have(second(p), p)
            elif p != 0:
                have("z1", p)
            block = grads.at[in_col(-p, 1 if kind == "z2" else 0)]
            to = in_col(d - p, 1 if kind in ("x", "dg") else 0)
            send(block, block, g_s[kind].at[d % NZ], g_r[kind].at[d % NZ], r, to)

    follow(GET_FIRST)
    wgrad = lax.dot_general(agg, grad, (((0,), (0,)), ((), ())), preferred_element_type=F32)
    bgrad = jnp.sum(grad.astype(F32).reshape(16, 8, SIDE), axis=0)
    own = [wgrad.reshape(N_ROW, 8, SIDE), jnp.broadcast_to(bgrad[None], (N_ROW, 8, SIDE))]
    ws[...] = jnp.concatenate(own, axis=1).astype(BF16)
    for k, (dy, dx, dk) in enumerate(ROW_PEERS):
        to = in_row(dy, dx, dk)
        send(ws.at[to], wr.at[k], w_s.at[k], w_r.at[k], to, c)

    act_out[...] = (pre * sig).astype(BF16)
    follow(GET_NEXT)
    total = ws[r].astype(F32)
    for k in range(len(ROW_PEERS)):
        landed(wr.at[k], w_r.at[k])
        total += wr[k].astype(F32)
    acc_a[...] = total.astype(BF16)
    for k, (dz, dh) in enumerate(ROUND_A):
        send(acc_a, wra.at[k], a_s.at[k], a_r.at[k], r, in_col(dz, dh))
    follow(GET_LAST)
    total = acc_a[...].astype(F32)
    for k in range(len(ROUND_A)):
        landed(wra.at[k], a_r.at[k])
        total += wra[k].astype(F32)
    acc_b[...] = total.astype(BF16)
    for k, (dz, dh) in enumerate(ROUND_B):
        send(acc_b, wrb.at[k], b_s.at[k], b_r.at[k], r, in_col(dz, dh))
    have("x", 0)
    for d in GET_PARENT:
        have("z1", d)
        have(second(d), d)

    def backward(t, carry):
        prod = jnp.dot(grads[tab[0, t]], tiles[t], preferred_element_type=F32)
        partial[t + 1] = prod + partial[tab[3, t]]
        return carry

    lax.fori_loop(0, SLOTS, backward, 0, unroll=True)

    for k, (dy, dx) in enumerate(CHIPS + ((0, 0),)):
        cs[k] = partial[tab[5, in_row(dy, dx, 1)]].astype(BF16)
        send(cs.at[k], cr.at[k], c_s.at[k], c_r.at[k], in_row(0, 0, 1), c)
    for k, (dy, dx) in enumerate(CHIPS):
        landed(cr.at[k], c_r.at[k])
        hs[k] = (partial[tab[5, in_row(dy, dx, 0)]] + cr[k].astype(F32)).astype(BF16)
        send(hs.at[k], hr.at[k], h_s.at[k], h_r.at[k], in_row(dy, dx, 0), c)

    total = acc_b[...].astype(F32)
    for k in range(len(ROUND_B)):
        landed(wrb.at[k], b_r.at[k])
        total += wrb[k].astype(F32)
    fin[r] = total[0:8]
    bg_out[...] = jnp.sum(total[8:16], axis=0, keepdims=True)
    for k, (dy, dx, dk) in enumerate(ROW_PEERS):
        send(fin.at[r], fin.at[r], e_s.at[k], e_r.at[k], in_row(dy, dx, dk), c)

    for copy in started[:-22]:
        copy.wait_send()
    del started[:-22]
    landed(cr.at[7], c_r.at[7])
    total = partial[tab[5, r]] + cr[7].astype(F32)
    for k in (6, 4, 5, 1, 2, 3, 0):
        landed(hr.at[k], h_r.at[k])
        total += hr[k].astype(F32)
    xg_out[...] = lax.dot_general(
        total.astype(BF16), weight[...], (((0,), (1,)), ((), ())), preferred_element_type=F32
    ).astype(BF16)
    for k, (dy, dx, dk) in enumerate(ROW_PEERS):
        landed(fin.at[in_row(4 - dy, dx, dk)], e_r.at[k])
    wg_out[...] = fin[...].reshape(SIDE, SIDE)
    for copy in started:
        copy.wait_send()


def finish(*refs):
    sem = refs[8]
    copies = [pltpu.make_async_copy(refs[k], refs[4 + k], sem.at[k]) for k in range(4)]
    for copy in copies:
        copy.start()
    for copy in copies:
        copy.wait()


def on_device(features, weight, bias, tile_values, tile_rows, tile_cols, tile_counts, out_grad):
    vmem = pl.BlockSpec(memory_space=pltpu.VMEM)
    dma = pltpu.SemaphoreType.DMA
    block = (SIDE, SIDE)
    hbm = pl.BlockSpec(memory_space=pltpu.HBM)

    def in_hbm(value):
        return pltpu.with_memory_space_constraint(value, pltpu.HBM)

    act, xg, wg, bg = pl.pallas_call(
        kernel,
        name="gcn",
        out_shape=(
            jax.ShapeDtypeStruct(block, BF16),
            jax.ShapeDtypeStruct(block, BF16),
            jax.ShapeDtypeStruct(block, F32),
            jax.ShapeDtypeStruct((1, SIDE), F32),
        ),
        in_specs=[hbm] * 8,
        out_specs=(vmem,) * 4,
        scratch_shapes=[
            pltpu.VMEM(block, BF16),
            pltpu.VMEM((1, SIDE), F32),
            pltpu.VMEM((1, SLOTS), jnp.int32),
            pltpu.VMEM((1, SLOTS), jnp.int32),
            pltpu.SMEM((1, 1), jnp.int32),
            pltpu.VMEM(block, BF16),
            pltpu.VMEM((SLOTS,) + block, BF16),
            pltpu.VMEM((N_ROW,) + block, BF16),
            pltpu.VMEM((SLOTS + 1,) + block, F32),
            pltpu.VMEM((N_COL,) + block, BF16),
            pltpu.VMEM((8, SIDE), jnp.int32),
            pltpu.SMEM((8, SIDE), jnp.int32),
            *[pltpu.VMEM((NZ,) + block, BF16)] * 7,
            pltpu.VMEM((8,) + block, BF16),
            pltpu.VMEM((8,) + block, BF16),
            pltpu.VMEM((7,) + block, BF16),
            pltpu.VMEM((7,) + block, BF16),
            pltpu.VMEM((N_ROW, 16, SIDE), BF16),
            pltpu.VMEM((15, 16, SIDE), BF16),
            pltpu.VMEM((16, SIDE), BF16),
            pltpu.VMEM((3, 16, SIDE), BF16),
            pltpu.VMEM((16, SIDE), BF16),
            pltpu.VMEM((7, 16, SIDE), BF16),
            pltpu.VMEM((N_ROW, 8, SIDE), F32),
            dma((9,)),
            pltpu.SemaphoreType.REGULAR,
            dma((8,)), dma((8,)), dma((7,)), dma((7,)),
            *[dma((NZ,))] * 16,
            dma((8,)), dma((8,)), dma((7,)), dma((7,)),
            dma((15,)), dma((15,)), dma((3,)), dma((3,)), dma((7,)), dma((7,)), dma((15,)), dma((15,)),
        ],
        compiler_params=pltpu.CompilerParams(
            collective_id=0, has_side_effects=True, vmem_limit_bytes=32 << 20
        ),
    )(
        *[in_hbm(v) for v in (features, weight, bias.reshape(1, SIDE), tile_values[0, 0], tile_rows[0], tile_cols[0])],
        tile_counts, in_hbm(out_grad),
    )
    act, xg, wg, bg = pl.pallas_call(
        finish,
        name="finish",
        out_shape=(
            jax.ShapeDtypeStruct(block, BF16),
            jax.ShapeDtypeStruct(block, BF16),
            jax.ShapeDtypeStruct(block, F32),
            jax.ShapeDtypeStruct((1, SIDE), F32),
        ),
        in_specs=[vmem] * 4,
        out_specs=(hbm,) * 4,
        scratch_shapes=[dma((4,))],
        compiler_params=pltpu.CompilerParams(vmem_limit_bytes=4 << 20),
    )(act, xg, wg, bg)
    return act, xg, wg, bg.reshape(SIDE)


def solution(mesh):
    return jax.shard_map(
        on_device,
        mesh=mesh,
        in_specs=(
            P(("row", "col"), None),
            P(),
            P(),
            P("row", "col", None, None, None),
            P("row", "col", None),
            P("row", "col", None),
            P("row", "col"),
            P(("row", "col"), None),
        ),
        out_specs=(P(("row", "col"), None), P(("row", "col"), None), P(), P()),
        check_vma=False,
    )
```

```python
import jax
import jax.numpy as jnp
from jax import lax
from jax.experimental import pallas as pl
from jax.experimental.pallas import tpu as pltpu
from jax.sharding import PartitionSpec as P

MESH = pl.DeviceIdType.MESH
F32 = jnp.float32
BF16 = jnp.bfloat16
SIDE = 128
SLOTS = 38
NY, NZ, NCORE = 4, 16, 2
N_ROW, N_COL = 16, 32

CHIPS = ((2, 1), (2, 0), (1, 1), (3, 1), (1, 0), (3, 0), (0, 1))
SUM_PARENT = {-7: -6, -6: 0, -5: -6, -4: -3, -3: -1, -2: -1, -1: 0, 1: 0, 2: 3, 3: 1, 4: 3, 5: 6, 6: 0, 7: 6, 8: 6}
SUM_BOTH = (-5, -4, 2, 3, 4, 5)
SUM_CROSS = (-3, 7)
SUM_PLAN = (('z2', -5), ('z2', 2), ('x', 8), ('z1', -4), ('z1', 4), ('z2', 5), ('x', -7), ('dg', 7), ('z2', 4), ('z1', 7), ('x', -2), ('z1', 5), ('z2', -4), ('z1', -5), ('z1', 2), ('x', 0), ('x', -1), ('x', -6), ('z1', 8), ('z1', -3), ('z1', -7), ('x', 6), ('z2', 3), ('z1', -2), ('dg', -3), ('z1', 3), ('z1', -6), ('z1', 6), ('x', 1), ('z1', -1), ('z1', 1))
GET_PARENT = {
    -7: -6, -6: 0, -5: -6, -4: -3, -3: -2, -2: 0, -1: -2, 1: 2, 2: 0, 3: 2, 4: 3, 5: 6, 6: 0, 7: 6, 8: 7,
}
GET_BOTH = (-7, -4, 1, 4, 7)
GET_CROSS = (-3, 3, 5, 8)
GET_FIRST = (("z1", 6), ("z1", -6), ("z1", 2), ("z1", -2), ("x", 0))
GET_NEXT = (
    ("dg", 3), ("z1", 3), ("x", 2), ("z1", 1), ("z1", -3), ("x", -2), ("dg", -3), ("z1", -1),
)
GET_LAST = (
    ("x", 6), ("z1", 7), ("dg", 5), ("z1", 5), ("z1", -7), ("x", -6), ("z1", -5), ("z2", 1), ("z1", 4), ("z1", -4),
    ("z2", 4), ("x", -1), ("dg", 8), ("z1", 8), ("z2", -4), ("x", -5), ("z2", 7), ("z2", -7),
)
ROUND_A = ((8, 0), (4, 0), (12, 0))
ROUND_B = ((2, 1), (1, 1), (15, 1), (2, 0), (0, 1), (1, 0), (15, 0))
ROW_PEERS = (
    (2, 1, 0), (2, 1, 1), (2, 0, 0), (2, 0, 1), (1, 1, 0), (3, 1, 0), (1, 1, 1), (3, 1, 1),
    (1, 0, 0), (3, 0, 0), (1, 0, 1), (3, 0, 1), (0, 1, 0), (0, 1, 1), (0, 0, 1),
)


def kernel(
    feat_hbm, weight_hbm, bias_hbm, tiles_hbm, rows_hbm, cols_hbm, counts_hbm, out_grad_hbm,
    act_out, xg_out, wg_out, bg_out,
    weight, bias, rows, cols, counts, out_grad, tiles, panel, partial, grads, table, tab,
    xs, xr, z1s, z1r, z2s, z2r, dgr, cs, cr, hs, hr, ws, wr, acc_a, wra, acc_b, wrb, fin,
    sem, ring, p_s, p_r, f_s, f_r, xs_s, xs_r, z1_s, z1_r, z2_s, z2_r, dg_s, dg_r,
    g1_s, g1_r, g2_s, g2_r, gd_s, gd_r, gx_s, gx_r,
    c_s, c_r, h_s, h_r, w_s, w_r, a_s, a_r, b_s, b_r, e_s, e_r,
):
    r = lax.axis_index("row")
    c = lax.axis_index("col")
    core, xl, y = r % 2, (r // 2) % 2, r // 4
    z, xh = c // 2, c % 2

    def in_row(dy, dx, dk):
        xx = xl + dx - 2 * xl * dx
        kk = core + dk - 2 * core * dk
        return ((y + dy) % NY) * 4 + xx * 2 + kk

    def in_col(dz, dh):
        hh = xh + dh - 2 * xh * dh
        return ((z + dz + NZ) % NZ) * 2 + hh

    def send(src, dst, ss, rs, row, col):
        copy = pltpu.make_async_remote_copy(
            src_ref=src, dst_ref=dst, send_sem=ss, recv_sem=rs, device_id=(row, col), device_id_type=MESH
        )
        copy.start()
        started.append(copy)

    def landed(dst, rs):
        pltpu.make_async_remote_copy(
            src_ref=dst, dst_ref=dst, send_sem=rs, recv_sem=rs, device_id=(r, c), device_id_type=MESH
        ).wait_recv()

    started = []
    g_s = {"z1": g1_s, "z2": g2_s, "dg": gd_s, "x": gx_s}
    g_r = {"z1": g1_r, "z2": g2_r, "dg": gd_r, "x": gx_r}
    barrier = pltpu.get_barrier_semaphore()
    greet = [(in_row(dy, dx, 0), c) for dy, dx in CHIPS[:1]] + [(r, in_col(d, 0)) for d in (3, -3, 2, -2)]
    greet += [(r, in_col(0, 1))] + [(in_row(dy, dx, 0), c) for dy, dx in CHIPS[1:]]
    greet += [(r, in_col(d, 0)) for d in (1, -1)] + [(in_row(0, 0, 1), c)]
    for row, col in greet:
        pl.semaphore_signal(barrier, inc=1, device_id=(row, col), device_id_type=MESH)

    fetch = [
        pltpu.make_async_copy(src, dst, sem.at[k])
        for k, (src, dst) in enumerate(
            (
                (feat_hbm, panel.at[r]), (rows_hbm, rows), (cols_hbm, cols), (counts_hbm, counts),
                (tiles_hbm, tiles), (weight_hbm, weight), (bias_hbm, bias), (out_grad_hbm, out_grad),
            )
        )
    ]
    for copy in fetch:
        copy.start()

    fetch[0].wait()
    pl.semaphore_wait(barrier, len(greet))

    for dz, dh in ((3, 0), (-3, 0), (0, 1)):
        pl.semaphore_signal(ring, inc=1, device_id=(r, in_col(dz, dh)), device_id_type=MESH)

    for k, (dy, dx) in enumerate(CHIPS):
        send(panel.at[r], panel.at[r], p_s.at[k], p_r.at[k], in_row(dy, dx, 0), c)
    send(panel.at[r], panel.at[r], p_s.at[7], p_r.at[7], in_row(0, 0, 1), c)
    for k in (1, 2, 3):
        fetch[k].wait()
    lane = lax.broadcasted_iota(jnp.int32, (SIDE, SIDE), 1)
    sub = lax.broadcasted_iota(jnp.int32, (SIDE, SIDE), 0)
    live = sub < counts[0, 0]
    for k, ref in ((0, rows), (1, cols)):
        padded = jnp.concatenate([ref[...], jnp.zeros((1, SIDE - SLOTS), jnp.int32)], axis=1)
        along = jnp.broadcast_to(padded, (SIDE, SIDE))
        down = jnp.sum(jnp.where(lane == sub, along, 0), axis=1, keepdims=True)
        down = jnp.broadcast_to(down, (SIDE, SIDE))
        prev = jnp.max(jnp.where((down == along) & (sub < lane) & live, sub + 1, 0), axis=0, keepdims=True)
        last = jnp.max(jnp.where((down == lane) & live, sub + 1, 0), axis=0, keepdims=True)
        table[k : k + 1, :] = padded
        table[2 + k : 3 + k, :] = prev
        table[4 + k : 5 + k, :] = last
    table[6:8, :] = jnp.zeros((2, SIDE), jnp.int32)
    to_scalar = pltpu.make_async_copy(table, tab, sem.at[8])
    to_scalar.start()
    partial[0] = jnp.zeros((SIDE, SIDE), F32)


    for k in (6, 4, 5, 1, 2, 3, 0):
        dy, dx = CHIPS[k]
        p = in_row(4 - dy, dx, 0)
        landed(panel.at[p], p_r.at[k])
        send(panel.at[p], panel.at[p], f_s.at[k], f_r.at[k], in_row(0, 0, 1), c)
    landed(panel.at[in_row(0, 0, 1)], p_r.at[7])
    to_scalar.wait()
    fetch[4].wait()
    for k, (dy, dx) in enumerate(CHIPS):
        landed(panel.at[in_row(4 - dy, dx, 1)], f_r.at[k])

    def forward(t, carry):
        prod = jnp.dot(tiles[t], panel[tab[1, t]], preferred_element_type=F32)
        partial[t + 1] = prod + partial[tab[2, t]]
        return carry

    lax.fori_loop(0, SLOTS, forward, 0, unroll=True)

    pl.semaphore_wait(ring, 3)

    def collect(e, kind):
        i = e % NZ
        own = in_col(-e, 0) if kind == "z1" else in_col(-e, 1)
        value = partial[tab[4, own]]
        for q in SUM_PARENT:
            if SUM_PARENT[q] == e and (kind == "z1" or q in SUM_BOTH):
                buf, got = (z1r, z1_r) if kind == "z1" else (z2r, z2_r)
                landed(buf.at[q % NZ], got.at[q % NZ])
                value += buf[q % NZ].astype(F32)
            if SUM_PARENT[q] == e and kind == "z1" and q in SUM_CROSS:
                landed(dgr.at[q % NZ], dg_r.at[q % NZ])
                value += dgr[q % NZ].astype(F32)
        if kind == "z1" and e not in SUM_BOTH + SUM_CROSS:
            landed(xr.at[i], xs_r.at[i])
            value += xr[i].astype(F32)
        return value

    for kind, e in SUM_PLAN:
        i = e % NZ
        value = collect(e, kind).astype(BF16)
        if kind == "x":
            xs[i] = value
            send(xs.at[i], xr.at[i], xs_s.at[i], xs_r.at[i], r, in_col(0, 1))
        elif kind == "z1":
            z1s[i] = value
            send(z1s.at[i], z1r.at[i], z1_s.at[i], z1_r.at[i], r, in_col(SUM_PARENT[e] - e, 0))
        elif kind == "dg":
            z2s[i] = value
            send(z2s.at[i], dgr.at[i], dg_s.at[i], dg_r.at[i], r, in_col(SUM_PARENT[e] - e, 1))
        else:
            z2s[i] = value
            send(z2s.at[i], z2r.at[i], z2_s.at[i], z2_r.at[i], r, in_col(SUM_PARENT[e] - e, 0))
    total = collect(0, "z1")

    for k in (5, 6, 7):
        fetch[k].wait()
    agg = total.astype(BF16)
    pre = jnp.dot(agg, weight[...], preferred_element_type=F32) + bias[...]
    sig = 1.0 / (1.0 + jnp.exp(-pre))
    grad = (out_grad[...].astype(F32) * (sig * (1.0 + pre * (1.0 - sig)))).astype(BF16)
    grads[c] = grad.T

    got = set()

    def have(kind, d):
        if (kind, d) not in got:
            got.add((kind, d))
            landed(grads.at[in_col(-d, 0 if kind == "z1" else 1)], g_r[kind].at[d % NZ])

    def second(d):
        return "z2" if d in GET_BOTH else "dg" if d in GET_CROSS else "x"

    def follow(plan):
        for kind, d in plan:
            p = d if kind == "x" else GET_PARENT[d]
            if kind == "z2":
                have(second(p), p)
            elif p != 0:
                have("z1", p)
            block = grads.at[in_col(-p, 1 if kind == "z2" else 0)]
            to = in_col(d - p, 1 if kind in ("x", "dg") else 0)
            send(block, block, g_s[kind].at[d % NZ], g_r[kind].at[d % NZ], r, to)

    follow(GET_FIRST)
    wgrad = lax.dot_general(agg, grad, (((0,), (0,)), ((), ())), preferred_element_type=F32)
    bgrad = jnp.sum(grad.astype(F32).reshape(16, 8, SIDE), axis=0)
    own = [wgrad.reshape(N_ROW, 8, SIDE), jnp.broadcast_to(bgrad[None], (N_ROW, 8, SIDE))]
    ws[...] = jnp.concatenate(own, axis=1).astype(BF16)
    for k, (dy, dx, dk) in enumerate(ROW_PEERS):
        to = in_row(dy, dx, dk)
        send(ws.at[to], wr.at[k], w_s.at[k], w_r.at[k], to, c)

    act_out[...] = (pre * sig).astype(BF16)
    follow(GET_NEXT)
    total = ws[r].astype(F32)
    for k in range(len(ROW_PEERS)):
        landed(wr.at[k], w_r.at[k])
        total += wr[k].astype(F32)
    acc_a[...] = total.astype(BF16)
    for k, (dz, dh) in enumerate(ROUND_A):
        send(acc_a, wra.at[k], a_s.at[k], a_r.at[k], r, in_col(dz, dh))
    follow(GET_LAST)
    total = acc_a[...].astype(F32)
    for k in range(len(ROUND_A)):
        landed(wra.at[k], a_r.at[k])
        total += wra[k].astype(F32)
    acc_b[...] = total.astype(BF16)
    for k, (dz, dh) in enumerate(ROUND_B):
        send(acc_b, wrb.at[k], b_s.at[k], b_r.at[k], r, in_col(dz, dh))
    have("x", 0)
    for d in GET_PARENT:
        have("z1", d)
        have(second(d), d)

    def backward(t, carry):
        prod = jnp.dot(grads[tab[0, t]], tiles[t], preferred_element_type=F32)
        partial[t + 1] = prod + partial[tab[3, t]]
        return carry

    lax.fori_loop(0, SLOTS, backward, 0, unroll=True)

    for k, (dy, dx) in enumerate(CHIPS + ((0, 0),)):
        cs[k] = partial[tab[5, in_row(dy, dx, 1)]].astype(BF16)
        send(cs.at[k], cr.at[k], c_s.at[k], c_r.at[k], in_row(0, 0, 1), c)
    for k, (dy, dx) in enumerate(CHIPS):
        landed(cr.at[k], c_r.at[k])
        hs[k] = (partial[tab[5, in_row(dy, dx, 0)]] + cr[k].astype(F32)).astype(BF16)
        send(hs.at[k], hr.at[k], h_s.at[k], h_r.at[k], in_row(dy, dx, 0), c)

    total = acc_b[...].astype(F32)
    for k in range(len(ROUND_B)):
        landed(wrb.at[k], b_r.at[k])
        total += wrb[k].astype(F32)
    fin[r] = total[0:8]
    bg_out[...] = jnp.sum(total[8:16], axis=0, keepdims=True)
    for k, (dy, dx, dk) in enumerate(ROW_PEERS):
        send(fin.at[r], fin.at[r], e_s.at[k], e_r.at[k], in_row(dy, dx, dk), c)

    for copy in started[:-22]:
        copy.wait_send()
    del started[:-22]
    landed(cr.at[7], c_r.at[7])
    total = partial[tab[5, r]] + cr[7].astype(F32)
    for k in (6, 4, 5, 1, 2, 3, 0):
        landed(hr.at[k], h_r.at[k])
        total += hr[k].astype(F32)
    xg_out[...] = lax.dot_general(
        total.astype(BF16), weight[...], (((0,), (1,)), ((), ())), preferred_element_type=F32
    ).astype(BF16)
    for k, (dy, dx, dk) in enumerate(ROW_PEERS):
        landed(fin.at[in_row(4 - dy, dx, dk)], e_r.at[k])
    wg_out[...] = fin[...].reshape(SIDE, SIDE)
    for copy in started:
        copy.wait_send()


def finish(*refs):
    sem = refs[8]
    copies = [pltpu.make_async_copy(refs[k], refs[4 + k], sem.at[k]) for k in range(4)]
    for copy in copies:
        copy.start()
    for copy in copies:
        copy.wait()


def on_device(features, weight, bias, tile_values, tile_rows, tile_cols, tile_counts, out_grad):
    vmem = pl.BlockSpec(memory_space=pltpu.VMEM)
    dma = pltpu.SemaphoreType.DMA
    block = (SIDE, SIDE)
    hbm = pl.BlockSpec(memory_space=pltpu.HBM)

    def in_hbm(value):
        return pltpu.with_memory_space_constraint(value, pltpu.HBM)

    act, xg, wg, bg = pl.pallas_call(
        kernel,
        name="gcn",
        out_shape=(
            jax.ShapeDtypeStruct(block, BF16),
            jax.ShapeDtypeStruct(block, BF16),
            jax.ShapeDtypeStruct(block, F32),
            jax.ShapeDtypeStruct((1, SIDE), F32),
        ),
        in_specs=[hbm] * 8,
        out_specs=(vmem,) * 4,
        scratch_shapes=[
            pltpu.VMEM(block, BF16),
            pltpu.VMEM((1, SIDE), F32),
            pltpu.VMEM((1, SLOTS), jnp.int32),
            pltpu.VMEM((1, SLOTS), jnp.int32),
            pltpu.SMEM((1, 1), jnp.int32),
            pltpu.VMEM(block, BF16),
            pltpu.VMEM((SLOTS,) + block, BF16),
            pltpu.VMEM((N_ROW,) + block, BF16),
            pltpu.VMEM((SLOTS + 1,) + block, F32),
            pltpu.VMEM((N_COL,) + block, BF16),
            pltpu.VMEM((8, SIDE), jnp.int32),
            pltpu.SMEM((8, SIDE), jnp.int32),
            *[pltpu.VMEM((NZ,) + block, BF16)] * 7,
            pltpu.VMEM((8,) + block, BF16),
            pltpu.VMEM((8,) + block, BF16),
            pltpu.VMEM((7,) + block, BF16),
            pltpu.VMEM((7,) + block, BF16),
            pltpu.VMEM((N_ROW, 16, SIDE), BF16),
            pltpu.VMEM((15, 16, SIDE), BF16),
            pltpu.VMEM((16, SIDE), BF16),
            pltpu.VMEM((3, 16, SIDE), BF16),
            pltpu.VMEM((16, SIDE), BF16),
            pltpu.VMEM((7, 16, SIDE), BF16),
            pltpu.VMEM((N_ROW, 8, SIDE), F32),
            dma((9,)),
            pltpu.SemaphoreType.REGULAR,
            dma((8,)), dma((8,)), dma((7,)), dma((7,)),
            *[dma((NZ,))] * 16,
            dma((8,)), dma((8,)), dma((7,)), dma((7,)),
            dma((15,)), dma((15,)), dma((3,)), dma((3,)), dma((7,)), dma((7,)), dma((15,)), dma((15,)),
        ],
        compiler_params=pltpu.CompilerParams(
            collective_id=0, has_side_effects=True, vmem_limit_bytes=32 << 20
        ),
    )(
        *[in_hbm(v) for v in (features, weight, bias.reshape(1, SIDE), tile_values[0, 0], tile_rows[0], tile_cols[0])],
        tile_counts, in_hbm(out_grad),
    )
    act, xg, wg, bg = pl.pallas_call(
        finish,
        name="finish",
        out_shape=(
            jax.ShapeDtypeStruct(block, BF16),
            jax.ShapeDtypeStruct(block, BF16),
            jax.ShapeDtypeStruct(block, F32),
            jax.ShapeDtypeStruct((1, SIDE), F32),
        ),
        in_specs=[vmem] * 4,
        out_specs=(hbm,) * 4,
        scratch_shapes=[dma((4,))],
        compiler_params=pltpu.CompilerParams(vmem_limit_bytes=4 << 20),
    )(act, xg, wg, bg)
    return act, xg, wg, bg.reshape(SIDE)


def solution(mesh):
    return jax.shard_map(
        on_device,
        mesh=mesh,
        in_specs=(
            P(("row", "col"), None),
            P(),
            P(),
            P("row", "col", None, None, None),
            P("row", "col", None),
            P("row", "col", None),
            P("row", "col"),
            P(("row", "col"), None),
        ),
        out_specs=(P(("row", "col"), None), P(("row", "col"), None), P(), P()),
        check_vma=False,
    )
```

```python
import jax
import jax.numpy as jnp
from jax import lax
from jax.experimental import pallas as pl
from jax.experimental.pallas import tpu as pltpu
from jax.sharding import PartitionSpec as P

MESH = pl.DeviceIdType.MESH
F32 = jnp.float32
BF16 = jnp.bfloat16
SIDE = 128
SLOTS = 38
NY, NZ, NCORE = 4, 16, 2
N_ROW, N_COL = 16, 32

CHIPS = ((2, 1), (2, 0), (1, 1), (3, 1), (1, 0), (3, 0), (0, 1))
SUM_PARENT = {-7: -6, -6: -4, -5: -4, -4: 0, -3: -2, -2: -1, -1: 0, 1: 0, 2: 1, 3: 2, 4: 0, 5: 4, 6: 4, 7: 6, 8: 6}
SUM_BOTH = (-7, -6, -3, -2, -1, 1, 2, 3, 7)
SUM_CROSS = ()
SUM_PLAN = (('x', 8), ('z2', -7), ('z2', -3), ('z1', -7), ('z2', 7), ('z2', 3), ('z1', 3), ('z1', 7), ('x', 5), ('x', -5), ('z1', -3), ('x', 4), ('z2', -6), ('z1', 8), ('x', 6), ('z2', -2), ('z2', 2), ('z1', -6), ('z1', 5), ('z1', 2), ('z1', -5), ('z1', -2), ('x', -4), ('z1', 6), ('z2', -1), ('z2', 1), ('z1', 1), ('z1', -1), ('z1', -4), ('z1', 4), ('x', 0))
GET_PARENT = {
    -7: -6, -6: 0, -5: -6, -4: -3, -3: -2, -2: 0, -1: -2, 1: 2, 2: 0, 3: 2, 4: 3, 5: 6, 6: 0, 7: 6, 8: 7,
}
GET_BOTH = (-7, -4, 1, 4, 7)
GET_CROSS = (-3, 3, 5, 8)
GET_FIRST = (("z1", 6), ("z1", -6), ("z1", 2), ("z1", -2), ("x", 0))
GET_NEXT = (
    ("dg", 3), ("z1", 3), ("x", 2), ("z1", 1), ("z1", -3), ("x", -2), ("dg", -3), ("z1", -1),
)
GET_LAST = (
    ("x", 6), ("z1", 7), ("dg", 5), ("z1", 5), ("z1", -7), ("x", -6), ("z1", -5), ("z2", 1), ("z1", 4), ("z1", -4),
    ("z2", 4), ("x", -1), ("dg", 8), ("z1", 8), ("z2", -4), ("x", -5), ("z2", 7), ("z2", -7),
)
ROUND_A = ((8, 0), (4, 0), (12, 0))
ROUND_B = ((2, 1), (1, 1), (15, 1), (2, 0), (0, 1), (1, 0), (15, 0))
ROW_PEERS = (
    (2, 1, 0), (2, 1, 1), (2, 0, 0), (2, 0, 1), (1, 1, 0), (3, 1, 0), (1, 1, 1), (3, 1, 1),
    (1, 0, 0), (3, 0, 0), (1, 0, 1), (3, 0, 1), (0, 1, 0), (0, 1, 1), (0, 0, 1),
)


def kernel(
    feat_hbm, weight_hbm, bias_hbm, tiles_hbm, rows_hbm, cols_hbm, counts_hbm, out_grad_hbm,
    act_out, xg_out, wg_out, bg_out,
    weight, bias, rows, cols, counts, out_grad, tiles, panel, partial, grads, table, tab,
    xs, xr, z1s, z1r, z2s, z2r, dgr, cs, cr, hs, hr, ws, wr, acc_a, wra, acc_b, wrb, fin,
    sem, ring, p_s, p_r, f_s, f_r, xs_s, xs_r, z1_s, z1_r, z2_s, z2_r, dg_s, dg_r,
    g1_s, g1_r, g2_s, g2_r, gd_s, gd_r, gx_s, gx_r,
    c_s, c_r, h_s, h_r, w_s, w_r, a_s, a_r, b_s, b_r, e_s, e_r,
):
    r = lax.axis_index("row")
    c = lax.axis_index("col")
    core, xl, y = r % 2, (r // 2) % 2, r // 4
    z, xh = c // 2, c % 2

    def in_row(dy, dx, dk):
        xx = xl + dx - 2 * xl * dx
        kk = core + dk - 2 * core * dk
        return ((y + dy) % NY) * 4 + xx * 2 + kk

    def in_col(dz, dh):
        hh = xh + dh - 2 * xh * dh
        return ((z + dz + NZ) % NZ) * 2 + hh

    def send(src, dst, ss, rs, row, col):
        copy = pltpu.make_async_remote_copy(
            src_ref=src, dst_ref=dst, send_sem=ss, recv_sem=rs, device_id=(row, col), device_id_type=MESH
        )
        copy.start()
        started.append(copy)

    def landed(dst, rs):
        pltpu.make_async_remote_copy(
            src_ref=dst, dst_ref=dst, send_sem=rs, recv_sem=rs, device_id=(r, c), device_id_type=MESH
        ).wait_recv()

    started = []
    g_s = {"z1": g1_s, "z2": g2_s, "dg": gd_s, "x": gx_s}
    g_r = {"z1": g1_r, "z2": g2_r, "dg": gd_r, "x": gx_r}
    barrier = pltpu.get_barrier_semaphore()
    greet = [(in_row(dy, dx, 0), c) for dy, dx in CHIPS[:1]] + [(r, in_col(d, 0)) for d in (3, -3, 2, -2)]
    greet += [(r, in_col(0, 1))] + [(in_row(dy, dx, 0), c) for dy, dx in CHIPS[1:]]
    greet += [(r, in_col(d, 0)) for d in (1, -1)] + [(in_row(0, 0, 1), c)]
    for row, col in greet:
        pl.semaphore_signal(barrier, inc=1, device_id=(row, col), device_id_type=MESH)

    fetch = [
        pltpu.make_async_copy(src, dst, sem.at[k])
        for k, (src, dst) in enumerate(
            (
                (feat_hbm, panel.at[r]), (rows_hbm, rows), (cols_hbm, cols), (counts_hbm, counts),
                (tiles_hbm, tiles), (weight_hbm, weight), (bias_hbm, bias), (out_grad_hbm, out_grad),
            )
        )
    ]
    for copy in fetch:
        copy.start()

    fetch[0].wait()
    pl.semaphore_wait(barrier, len(greet))

    for dz, dh in ((3, 0), (-3, 0), (0, 1)):
        pl.semaphore_signal(ring, inc=1, device_id=(r, in_col(dz, dh)), device_id_type=MESH)

    for k, (dy, dx) in enumerate(CHIPS):
        send(panel.at[r], panel.at[r], p_s.at[k], p_r.at[k], in_row(dy, dx, 0), c)
    send(panel.at[r], panel.at[r], p_s.at[7], p_r.at[7], in_row(0, 0, 1), c)
    for k in (1, 2, 3):
        fetch[k].wait()
    lane = lax.broadcasted_iota(jnp.int32, (SIDE, SIDE), 1)
    sub = lax.broadcasted_iota(jnp.int32, (SIDE, SIDE), 0)
    live = sub < counts[0, 0]
    for k, ref in ((0, rows), (1, cols)):
        padded = jnp.concatenate([ref[...], jnp.zeros((1, SIDE - SLOTS), jnp.int32)], axis=1)
        along = jnp.broadcast_to(padded, (SIDE, SIDE))
        down = jnp.sum(jnp.where(lane == sub, along, 0), axis=1, keepdims=True)
        down = jnp.broadcast_to(down, (SIDE, SIDE))
        prev = jnp.max(jnp.where((down == along) & (sub < lane) & live, sub + 1, 0), axis=0, keepdims=True)
        last = jnp.max(jnp.where((down == lane) & live, sub + 1, 0), axis=0, keepdims=True)
        table[k : k + 1, :] = padded
        table[2 + k : 3 + k, :] = prev
        table[4 + k : 5 + k, :] = last
    table[6:8, :] = jnp.zeros((2, SIDE), jnp.int32)
    to_scalar = pltpu.make_async_copy(table, tab, sem.at[8])
    to_scalar.start()
    partial[0] = jnp.zeros((SIDE, SIDE), F32)


    for k in (6, 4, 5, 1, 2, 3, 0):
        dy, dx = CHIPS[k]
        p = in_row(4 - dy, dx, 0)
        landed(panel.at[p], p_r.at[k])
        send(panel.at[p], panel.at[p], f_s.at[k], f_r.at[k], in_row(0, 0, 1), c)
    landed(panel.at[in_row(0, 0, 1)], p_r.at[7])
    to_scalar.wait()
    fetch[4].wait()
    for k, (dy, dx) in enumerate(CHIPS):
        landed(panel.at[in_row(4 - dy, dx, 1)], f_r.at[k])

    def forward(t, carry):
        prod = jnp.dot(tiles[t], panel[tab[1, t]], preferred_element_type=F32)
        partial[t + 1] = prod + partial[tab[2, t]]
        return carry

    lax.fori_loop(0, SLOTS, forward, 0, unroll=True)

    pl.semaphore_wait(ring, 3)

    def collect(e, kind):
        i = e % NZ
        own = in_col(-e, 0) if kind == "z1" else in_col(-e, 1)
        value = partial[tab[4, own]]
        for q in SUM_PARENT:
            if SUM_PARENT[q] == e and (kind == "z1" or q in SUM_BOTH):
                buf, got = (z1r, z1_r) if kind == "z1" else (z2r, z2_r)
                landed(buf.at[q % NZ], got.at[q % NZ])
                value += buf[q % NZ].astype(F32)
            if SUM_PARENT[q] == e and kind == "z1" and q in SUM_CROSS:
                landed(dgr.at[q % NZ], dg_r.at[q % NZ])
                value += dgr[q % NZ].astype(F32)
        if kind == "z1" and e not in SUM_BOTH + SUM_CROSS:
            landed(xr.at[i], xs_r.at[i])
            value += xr[i].astype(F32)
        return value

    for kind, e in SUM_PLAN:
        i = e % NZ
        value = collect(e, kind).astype(BF16)
        if kind == "x":
            xs[i] = value
            send(xs.at[i], xr.at[i], xs_s.at[i], xs_r.at[i], r, in_col(0, 1))
        elif kind == "z1":
            z1s[i] = value
            send(z1s.at[i], z1r.at[i], z1_s.at[i], z1_r.at[i], r, in_col(SUM_PARENT[e] - e, 0))
        elif kind == "dg":
            z2s[i] = value
            send(z2s.at[i], dgr.at[i], dg_s.at[i], dg_r.at[i], r, in_col(SUM_PARENT[e] - e, 1))
        else:
            z2s[i] = value
            send(z2s.at[i], z2r.at[i], z2_s.at[i], z2_r.at[i], r, in_col(SUM_PARENT[e] - e, 0))
    total = collect(0, "z1")

    for k in (5, 6, 7):
        fetch[k].wait()
    agg = total.astype(BF16)
    pre = jnp.dot(agg, weight[...], preferred_element_type=F32) + bias[...]
    sig = 1.0 / (1.0 + jnp.exp(-pre))
    grad = (out_grad[...].astype(F32) * (sig * (1.0 + pre * (1.0 - sig)))).astype(BF16)
    grads[c] = grad.T

    got = set()

    def have(kind, d):
        if (kind, d) not in got:
            got.add((kind, d))
            landed(grads.at[in_col(-d, 0 if kind == "z1" else 1)], g_r[kind].at[d % NZ])

    def second(d):
        return "z2" if d in GET_BOTH else "dg" if d in GET_CROSS else "x"

    def follow(plan):
        for kind, d in plan:
            p = d if kind == "x" else GET_PARENT[d]
            if kind == "z2":
                have(second(p), p)
            elif p != 0:
                have("z1", p)
            block = grads.at[in_col(-p, 1 if kind == "z2" else 0)]
            to = in_col(d - p, 1 if kind in ("x", "dg") else 0)
            send(block, block, g_s[kind].at[d % NZ], g_r[kind].at[d % NZ], r, to)

    follow(GET_FIRST)
    wgrad = lax.dot_general(agg, grad, (((0,), (0,)), ((), ())), preferred_element_type=F32)
    bgrad = jnp.sum(grad.astype(F32).reshape(16, 8, SIDE), axis=0)
    own = [wgrad.reshape(N_ROW, 8, SIDE), jnp.broadcast_to(bgrad[None], (N_ROW, 8, SIDE))]
    ws[...] = jnp.concatenate(own, axis=1).astype(BF16)
    for k, (dy, dx, dk) in enumerate(ROW_PEERS):
        to = in_row(dy, dx, dk)
        send(ws.at[to], wr.at[k], w_s.at[k], w_r.at[k], to, c)

    act_out[...] = (pre * sig).astype(BF16)
    follow(GET_NEXT)
    total = ws[r].astype(F32)
    for k in range(len(ROW_PEERS)):
        landed(wr.at[k], w_r.at[k])
        total += wr[k].astype(F32)
    acc_a[...] = total.astype(BF16)
    for k, (dz, dh) in enumerate(ROUND_A):
        send(acc_a, wra.at[k], a_s.at[k], a_r.at[k], r, in_col(dz, dh))
    follow(GET_LAST)
    total = acc_a[...].astype(F32)
    for k in range(len(ROUND_A)):
        landed(wra.at[k], a_r.at[k])
        total += wra[k].astype(F32)
    acc_b[...] = total.astype(BF16)
    for k, (dz, dh) in enumerate(ROUND_B):
        send(acc_b, wrb.at[k], b_s.at[k], b_r.at[k], r, in_col(dz, dh))
    have("x", 0)
    for d in GET_PARENT:
        have("z1", d)
        have(second(d), d)

    def backward(t, carry):
        prod = jnp.dot(grads[tab[0, t]], tiles[t], preferred_element_type=F32)
        partial[t + 1] = prod + partial[tab[3, t]]
        return carry

    lax.fori_loop(0, SLOTS, backward, 0, unroll=True)

    for k, (dy, dx) in enumerate(CHIPS + ((0, 0),)):
        cs[k] = partial[tab[5, in_row(dy, dx, 1)]].astype(BF16)
        send(cs.at[k], cr.at[k], c_s.at[k], c_r.at[k], in_row(0, 0, 1), c)
    for k, (dy, dx) in enumerate(CHIPS):
        landed(cr.at[k], c_r.at[k])
        hs[k] = (partial[tab[5, in_row(dy, dx, 0)]] + cr[k].astype(F32)).astype(BF16)
        send(hs.at[k], hr.at[k], h_s.at[k], h_r.at[k], in_row(dy, dx, 0), c)

    total = acc_b[...].astype(F32)
    for k in range(len(ROUND_B)):
        landed(wrb.at[k], b_r.at[k])
        total += wrb[k].astype(F32)
    fin[r] = total[0:8]
    bg_out[...] = jnp.sum(total[8:16], axis=0, keepdims=True)
    for k, (dy, dx, dk) in enumerate(ROW_PEERS):
        send(fin.at[r], fin.at[r], e_s.at[k], e_r.at[k], in_row(dy, dx, dk), c)

    for copy in started[:-22]:
        copy.wait_send()
    del started[:-22]
    landed(cr.at[7], c_r.at[7])
    total = partial[tab[5, r]] + cr[7].astype(F32)
    for k in (6, 4, 5, 1, 2, 3, 0):
        landed(hr.at[k], h_r.at[k])
        total += hr[k].astype(F32)
    xg_out[...] = lax.dot_general(
        total.astype(BF16), weight[...], (((0,), (1,)), ((), ())), preferred_element_type=F32
    ).astype(BF16)
    for k, (dy, dx, dk) in enumerate(ROW_PEERS):
        landed(fin.at[in_row(4 - dy, dx, dk)], e_r.at[k])
    wg_out[...] = fin[...].reshape(SIDE, SIDE)
    for copy in started:
        copy.wait_send()


def finish(*refs):
    sem = refs[8]
    copies = [pltpu.make_async_copy(refs[k], refs[4 + k], sem.at[k]) for k in range(4)]
    for copy in copies:
        copy.start()
    for copy in copies:
        copy.wait()


def on_device(features, weight, bias, tile_values, tile_rows, tile_cols, tile_counts, out_grad):
    vmem = pl.BlockSpec(memory_space=pltpu.VMEM)
    dma = pltpu.SemaphoreType.DMA
    block = (SIDE, SIDE)
    hbm = pl.BlockSpec(memory_space=pltpu.HBM)

    def in_hbm(value):
        return pltpu.with_memory_space_constraint(value, pltpu.HBM)

    act, xg, wg, bg = pl.pallas_call(
        kernel,
        name="gcn",
        out_shape=(
            jax.ShapeDtypeStruct(block, BF16),
            jax.ShapeDtypeStruct(block, BF16),
            jax.ShapeDtypeStruct(block, F32),
            jax.ShapeDtypeStruct((1, SIDE), F32),
        ),
        in_specs=[hbm] * 8,
        out_specs=(vmem,) * 4,
        scratch_shapes=[
            pltpu.VMEM(block, BF16),
            pltpu.VMEM((1, SIDE), F32),
            pltpu.VMEM((1, SLOTS), jnp.int32),
            pltpu.VMEM((1, SLOTS), jnp.int32),
            pltpu.SMEM((1, 1), jnp.int32),
            pltpu.VMEM(block, BF16),
            pltpu.VMEM((SLOTS,) + block, BF16),
            pltpu.VMEM((N_ROW,) + block, BF16),
            pltpu.VMEM((SLOTS + 1,) + block, F32),
            pltpu.VMEM((N_COL,) + block, BF16),
            pltpu.VMEM((8, SIDE), jnp.int32),
            pltpu.SMEM((8, SIDE), jnp.int32),
            *[pltpu.VMEM((NZ,) + block, BF16)] * 7,
            pltpu.VMEM((8,) + block, BF16),
            pltpu.VMEM((8,) + block, BF16),
            pltpu.VMEM((7,) + block, BF16),
            pltpu.VMEM((7,) + block, BF16),
            pltpu.VMEM((N_ROW, 16, SIDE), BF16),
            pltpu.VMEM((15, 16, SIDE), BF16),
            pltpu.VMEM((16, SIDE), BF16),
            pltpu.VMEM((3, 16, SIDE), BF16),
            pltpu.VMEM((16, SIDE), BF16),
            pltpu.VMEM((7, 16, SIDE), BF16),
            pltpu.VMEM((N_ROW, 8, SIDE), F32),
            dma((9,)),
            pltpu.SemaphoreType.REGULAR,
            dma((8,)), dma((8,)), dma((7,)), dma((7,)),
            *[dma((NZ,))] * 16,
            dma((8,)), dma((8,)), dma((7,)), dma((7,)),
            dma((15,)), dma((15,)), dma((3,)), dma((3,)), dma((7,)), dma((7,)), dma((15,)), dma((15,)),
        ],
        compiler_params=pltpu.CompilerParams(
            collective_id=0, has_side_effects=True, vmem_limit_bytes=32 << 20
        ),
    )(
        *[in_hbm(v) for v in (features, weight, bias.reshape(1, SIDE), tile_values[0, 0], tile_rows[0], tile_cols[0])],
        tile_counts, in_hbm(out_grad),
    )
    act, xg, wg, bg = pl.pallas_call(
        finish,
        name="finish",
        out_shape=(
            jax.ShapeDtypeStruct(block, BF16),
            jax.ShapeDtypeStruct(block, BF16),
            jax.ShapeDtypeStruct(block, F32),
            jax.ShapeDtypeStruct((1, SIDE), F32),
        ),
        in_specs=[vmem] * 4,
        out_specs=(hbm,) * 4,
        scratch_shapes=[dma((4,))],
        compiler_params=pltpu.CompilerParams(vmem_limit_bytes=4 << 20),
    )(act, xg, wg, bg)
    return act, xg, wg, bg.reshape(SIDE)


def solution(mesh):
    return jax.shard_map(
        on_device,
        mesh=mesh,
        in_specs=(
            P(("row", "col"), None),
            P(),
            P(),
            P("row", "col", None, None, None),
            P("row", "col", None),
            P("row", "col", None),
            P("row", "col"),
            P(("row", "col"), None),
        ),
        out_specs=(P(("row", "col"), None), P(("row", "col"), None), P(), P()),
        check_vma=False,
    )
```
